32 devices in a mesh: seq: 4 (over y, core), users: 8 (over z, x).
Axes of the slice: x: 2, y: 2, z: 4, core: 2. Of those that a mesh axis runs over, the one named last changes fastest.
Arguments:
- hidden: float32 [8, 4096, 512], P('users', 'seq'), may hold values from -256 to 256
- target: bfloat16 [8, 4096, 512], P('users', 'seq'), may hold values from -0.25 to 0.25
- pool_table: bfloat16 [8192, 512], P('users'), may hold values from -1 to 1
- pool_items: int32 [8192], P('users'), may hold values from 1 to 16383
- labels: int32 [8, 4096], P('users', 'seq'), may hold values from 1 to 16383
- chosen: int32 [8, 32, 8], P('users', 'seq'), may hold values from 0 to 31, all different within a row
- offsets: int32 [8, 5], P('users'), may hold values from 0 to 4096, as said below
Outputs:
- loss: float32 [], replicated
- grad_hidden: float32 [8, 4096, 512], P('users', 'seq')
- grad_table: float32 [8192, 512], P('users')
The draws below stay inside these ranges and needn't reach their ends.
Inputs may be any that keep to these rules, and one draw needn't show every extreme that they name: Each row offsets[u] starts at 0 and rises strictly; its last entry is the number of live positions of group u, and equals 4096 in some group; positions from it on are padding. `chosen`: each position block names 8 different negative blocks.
All inputs are finite; a program needn't handle non-finite values.
Results may differ from the reference program's by a relative error of at most 0.003.
Values may be sent and summed in bfloat16 or wider, within the bound.
No kernel may reach another device: no remote copies, remote signals or barrier semaphores. Data moves between devices by JAX's collectives and lax.ppermute only.
A program may use at most 192 MiB of HBM per device.

```python
import math
import jax
import jax.numpy as jnp
from jax import lax

D = 512
NEG = 8192
NB = 256
KB = 8
PB = 128
HISTS = 4
ITEMS = 16384
USER_GROUPS = 8
GROUP_ROWS = 4096
GROUP_BLOCKS = 32
NEG_BLOCKS = 32


def common_direction(key):
    sub_key = jax.random.fold_in(key, 911)
    return jax.random.truncated_normal(sub_key, -3.0, 3.0, (D,), jnp.float32) / math.sqrt(D)


def draw_pool_table(key, part):
    direction = common_direction(key)
    key_base, key_hot = jax.random.split(jax.random.fold_in(key, 912), 2)
    base = jax.random.truncated_normal(key_base, -4.0, 4.0, (NEG, D), jnp.float32) / math.sqrt(D)
    hot_slot = jax.random.randint(key_hot, (NEG // NB,), 0, NB)
    is_hot = (jnp.arange(NB)[None, :] == hot_slot[:, None]).reshape(NEG, 1)
    rows = jnp.where(is_hot, direction[None, :] + 0.15 * base, base)
    return jnp.clip(rows, -1.0, 1.0).astype(jnp.bfloat16)


def draw_hidden(key, part):
    direction = common_direction(key)
    key_base, key_pick, key_power = jax.random.split(jax.random.fold_in(key, 913), 3)
    base = jax.random.truncated_normal(key_base, -6.0, 6.0, (USER_GROUPS, GROUP_ROWS, D), jnp.float32)
    planted = jax.random.randint(key_pick, (USER_GROUPS, GROUP_ROWS, 1), 0, 64) == 0
    power = jax.random.uniform(key_power, (USER_GROUPS, GROUP_ROWS, 1), jnp.float32, 120.0, 360.0)
    rows = jnp.where(planted, power * direction[None, None, :] + 0.05 * base, base)
    return jnp.clip(rows, -256.0, 256.0).astype(jnp.float32)


def draw_offsets(key, part):
    ceiling = GROUP_ROWS
    key_len, key_full, key_cut = jax.random.split(key, 3)
    totals = jax.random.randint(key_len, (USER_GROUPS,), ceiling // 8, ceiling + 1)
    fullest = jax.random.randint(key_full, (), 0, USER_GROUPS)
    totals = jnp.where(jnp.arange(USER_GROUPS) == fullest, ceiling, totals).astype(jnp.int32)
    draws_raw = jax.random.randint(key_cut, (USER_GROUPS, HISTS - 1), 0, 1 << 30)
    cut_points = draws_raw % (totals[:, None] - HISTS + 1)
    cut_points = jnp.sort(cut_points, axis=1) + jnp.arange(1, HISTS, dtype=jnp.int32)[None, :]
    leading = jnp.zeros((USER_GROUPS, 1), jnp.int32)
    return jnp.concatenate([leading, cut_points.astype(jnp.int32), totals[:, None]], axis=1).astype(jnp.int32)


def place_ends(array, own_key, smallest, largest):
    dims = array.shape
    place = [jax.random.randint(jax.random.fold_in(own_key, axis), (), 0, dims[axis]) for axis in range(len(dims))]
    array = array.at[tuple(place)].set(smallest)
    longest = dims.index(max(dims))
    place[longest] = (place[longest] + 1) % dims[longest]
    return array.at[tuple(place)].set(largest)


def levels(own_key, shape, cuts, low, top_value):
    def one(dim, parts):
        draws = jax.random.uniform(jax.random.fold_in(jax.random.fold_in(own_key, 6), dim), (parts,), jnp.float32, low / len(cuts), top_value / len(cuts))
        return jnp.repeat(jnp.exp(draws), shape[dim] // parts).reshape((-1,) + (1,) * (len(shape) - dim - 1))

    loudness = one(*cuts[0])
    for cut in cuts[1:]:
        loudness = loudness * one(*cut)
    return loudness


def choose_distinct(key, rows, count, top, lift):
    sequence = jax.random.permutation(jax.random.fold_in(key, 1), count)
    boost = sequence
    for power in range(3):
        boost = boost * boost // count
    boost = boost * lift // count
    lots = jax.random.randint(jax.random.fold_in(key, 2), (rows, count), 0, 4096) + boost
    sure = jax.random.permutation(jax.random.fold_in(key, 3), rows)[jnp.arange(count) % rows]
    lots = jnp.where(jnp.arange(rows)[:, None] == sure[None, :], 1 << 14, lots)
    score = lots * count + jnp.arange(count)
    return lax.top_k(score.astype(jnp.int32), top)[1].astype(jnp.int32)


def gaussian(rng, extent, scale, bound, cuts=(), kind=jnp.bfloat16):
    result = scale * jax.random.normal(rng, extent, jnp.float32)
    if cuts:
        result = result * levels(rng, extent, cuts, -0.22, 0.18)
    return jnp.clip(result, -bound, bound).astype(kind)


def setup_inputs(seed: int = 0) -> dict:
    splits = jax.random.split(jax.random.key(seed), 8)
    hidden = draw_hidden(jax.random.fold_in(splits[7], 71), 0)
    target = gaussian(splits[1], (USER_GROUPS, GROUP_ROWS, D), D ** -0.5, 0.25, ((0, 8), (1, 4)))
    pool_table = draw_pool_table(jax.random.fold_in(splits[7], 71), 0)
    pool_items = place_ends(jax.random.randint(splits[3], (NEG,), 1, ITEMS), jax.random.fold_in(splits[3], 1), 1, ITEMS - 1).astype(jnp.int32)
    labels = place_ends(jax.random.randint(splits[4], (USER_GROUPS, GROUP_ROWS), 1, ITEMS), jax.random.fold_in(splits[4], 1), 1, ITEMS - 1).astype(jnp.int32)
    chosen = choose_distinct(splits[5], USER_GROUPS * GROUP_BLOCKS, NEG_BLOCKS, KB, 2048).reshape((USER_GROUPS, GROUP_BLOCKS, KB))
    offsets = draw_offsets(jax.random.fold_in(splits[7], 71), 0)
    return dict(hidden=hidden, target=target, pool_table=pool_table, pool_items=pool_items, labels=labels, chosen=chosen, offsets=offsets)


def history_weights(bounds, positions):
    starts = bounds[:-1]
    finish = bounds[1:]
    lengths = (finish - starts).astype(jnp.float32)
    inside = (positions[..., None] >= starts) & (positions[..., None] < finish)
    return jnp.sum(jnp.where(inside, 1.0 / lengths, 0.0), axis=-1).astype(jnp.float32)


def block_terms(states, target, labels, weights, chosen, pool_rows, pool_ids, factor):
    narrow = states.astype(jnp.bfloat16)
    negatives = jnp.take(pool_rows, chosen, axis=0).reshape(-1, pool_rows.shape[2])
    neg_items = jnp.take(pool_ids, chosen, axis=0).reshape(-1)
    scores = jnp.dot(narrow, negatives.T, preferred_element_type=jnp.float32)
    target_wide = target.astype(jnp.float32)
    positive = jnp.sum(narrow.astype(jnp.float32) * target_wide, axis=1)
    masked = jnp.where(neg_items[None, :] == labels[:, None], -1e30, scores)
    peak = jnp.maximum(positive, jnp.max(masked, axis=1))
    neg_exp = jnp.exp(masked - peak[:, None])
    pos_exp = jnp.exp(positive - peak)
    totals = pos_exp + jnp.sum(neg_exp, axis=1)
    cross = peak + jnp.log(totals) - positive
    coeff = weights * factor
    neg_grad = (coeff[:, None] * neg_exp / totals[:, None]).astype(jnp.bfloat16)
    pos_grad = coeff * (pos_exp / totals - 1.0)
    state_grad = jnp.dot(neg_grad, negatives, preferred_element_type=jnp.float32) + pos_grad[:, None] * target_wide
    pool_grad = jnp.dot(neg_grad.T, narrow, preferred_element_type=jnp.float32)
    pool_grad = pool_grad.reshape(chosen.shape[0], pool_rows.shape[1], pool_rows.shape[2])
    return jnp.sum(weights * cross), state_grad, pool_grad


def reference(hidden, target, pool_table, pool_items, labels, chosen, offsets):
    groups = hidden.shape[0]
    length = hidden.shape[1]
    positions = jnp.arange(length, dtype=jnp.int32)
    weights = jax.vmap(history_weights, in_axes=(0, None))(offsets, positions)
    factor = 1.0 / (groups * (offsets.shape[1] - 1))
    pool_rows = pool_table.reshape(NEG // NB, NB, D)
    pool_ids = pool_items.reshape(NEG // NB, NB)
    sliced = (hidden.reshape(-1, PB, D), target.reshape(-1, PB, D), labels.reshape(-1, PB),
              weights.reshape(-1, PB), chosen.reshape(-1, KB))

    def advance(carried, slices):
        loss_acc, grad_acc = carried
        part_loss, state_grad, pool_grad = block_terms(slices[0], slices[1], slices[2], slices[3], slices[4], pool_rows, pool_ids, factor)
        return (loss_acc + part_loss, grad_acc.at[slices[4]].add(pool_grad)), state_grad

    initial = (jnp.zeros((), jnp.float32), jnp.zeros((NEG // NB, NB, D), jnp.float32))
    (loss_acc, grad_acc), state_grads = lax.scan(advance, initial, sliced)
    return loss_acc * factor, state_grads.reshape(hidden.shape), grad_acc.reshape(NEG, D)
```

```python
import functools
import jax
import jax.numpy as jnp
from jax import lax
from jax.experimental import pallas as pl
from jax.experimental.pallas import tpu as pltpu
from jax.sharding import PartitionSpec as P

NB = 256
PB = 128
HEAD = 16
ID_BASE = 128
VMEM = 48 * 1024 * 1024
NT = (((1,), (1,)), ((), ()))
TN = (((0,), (0,)), ((), ()))


def swap(array, axis, mask):
    count = lax.axis_size(axis)
    return lax.ppermute(array, axis, [(i, i ^ mask) for i in range(count)])


def history_weights(bounds, positions):
    starts = bounds[:-1]
    finish = bounds[1:]
    lengths = (finish - starts).astype(jnp.float32)
    inside = (positions[..., None] >= starts) & (positions[..., None] < finish)
    return jnp.sum(jnp.where(inside, 1.0 / lengths, 0.0), axis=-1)


def gather_slabs(table, index, first, count, per_piece, stride, slab):
    rows = []
    for k in range(count):
        base = index[first + k]
        row = (base // per_piece) * stride + (base % per_piece) * slab
        rows.append(table[pl.ds(pl.multiple_of(row, 16), slab), :])
    return rows


def lane_row(columns):
    folded = columns[:, :PB]
    for k in range(1, columns.shape[1] // PB):
        folded = folded + columns[:, k * PB:(k + 1) * PB]
    return jnp.sum(folded.T, axis=0, keepdims=True)


def load_pieces(pieces, table, sems, stride):
    copies = [
        pltpu.make_async_copy(piece, table.at[pl.ds(k * stride, stride)], sems.at[k])
        for k, piece in enumerate(pieces)
    ]
    for copy in copies:
        copy.start()
    for copy in copies:
        copy.wait()


def score_kernel(dims, index, *refs):
    peers, blocks, picks, users, per_piece, slab = dims
    labels, narrows, target = refs[0], refs[1:1 + peers], refs[1 + peers]
    pieces = refs[2 + peers:2 + peers + users]
    scores, stats, positives, table, items, sems = refs[2 + peers + users:]
    rows = per_piece * slab
    stride = rows + HEAD
    step = pl.program_id(0)

    @pl.when(step == 0)
    def _():
        load_pieces(pieces, table, sems, stride)
        place = lax.broadcasted_iota(jnp.int32, (HEAD, PB), 0)
        units = jnp.where(place == 0, float(ID_BASE), jnp.where(place == 1, 1.0, 0.0)).astype(jnp.bfloat16)
        top = jnp.zeros((1, PB), jnp.float32)
        for k in range(users):
            head = table[pl.ds(k * stride + rows, HEAD), :]
            items[pl.ds(k * stride, rows), :] = lax.dot_general(
                head[:, :rows], units, TN, preferred_element_type=jnp.float32
            )
            top = jnp.maximum(top, head.astype(jnp.float32)[2:3, :PB])
        stats[pl.ds(2 * peers * blocks, 8), :] = jnp.broadcast_to(top, (8, PB))

    for r in range(peers):
        first = (r * blocks + step) * picks
        narrow = narrows[r][...]
        candidates = jnp.concatenate(gather_slabs(table, index, first, picks, per_piece, stride, slab), axis=0)
        ids = jnp.concatenate(gather_slabs(items, index, first, picks, per_piece, stride, slab), axis=0)
        score = lax.dot_general(candidates, narrow, NT, preferred_element_type=jnp.float32)
        masked = jnp.where(ids == labels[0, pl.ds(r, 1), :], -1e30, score)
        scores[0, r] = masked
        peak = jnp.max(masked, axis=0, keepdims=True)
        total = jnp.sum(jnp.exp(masked - peak), axis=0, keepdims=True)
        if r == 0:
            positive = lane_row(narrow.astype(jnp.float32) * target[...].astype(jnp.float32))
            positives[pl.ds(step, 1), :] = positive
            higher = jnp.maximum(peak, positive)
            total = total * jnp.exp(peak - higher) + jnp.exp(positive - higher)
            peak = higher
        stats[pl.ds(r * blocks + step, 1), :] = peak
        stats[pl.ds((peers + r) * blocks + step, 1), :] = total


def table_kernel(dims, index, *refs):
    peers, blocks, picks, users, per_piece, slab, factor = dims
    scores, weights, positives = refs[:3]
    stats = refs[3:3 + peers]
    narrows = refs[3 + peers:3 + 2 * peers]
    grads, partial, pos_grad, losses, bound, peaks, ratios = refs[3 + 2 * peers:]
    step = pl.program_id(0)

    @pl.when(step == 0)
    def _():
        partial[...] = jnp.zeros_like(partial)
        for r in range(peers):
            tops = [stats[q][pl.ds((q ^ r) * blocks, blocks), :] for q in range(peers)]
            sums = [stats[q][pl.ds((peers + (q ^ r)) * blocks, blocks), :] for q in range(peers)]
            peak = functools.reduce(jnp.maximum, tops)
            total = functools.reduce(jnp.add, [s * jnp.exp(t - peak) for t, s in zip(tops, sums)])
            weight = weights[r]
            peaks[pl.ds(r * blocks, blocks), :] = peak
            ratios[pl.ds(r * blocks, blocks), :] = weight * factor / total
            if r == 0:
                positive = positives[...]
                pos_grad[...] = weight * factor * (jnp.exp(positive - peak) / total - 1.0)
                losses[...] = weight * (peak + jnp.log(total) - positive)
        bound[...] = functools.reduce(jnp.maximum, [s[pl.ds(2 * peers * blocks, 8), :] for s in stats])

    for r in range(peers):
        first = (r * blocks + step) * picks
        peak = peaks[pl.ds(r * blocks + step, 1), :]
        ratio = ratios[pl.ds(r * blocks + step, 1), :]
        grad = (jnp.exp(scores[0, r] - peak) * ratio).astype(jnp.bfloat16)
        grads[0, r] = grad
        rows = jnp.dot(grad, narrows[r][...], preferred_element_type=jnp.float32)
        for k in range(picks):
            place = pl.ds(pl.multiple_of(index[first + k] * slab, 16), slab)
            partial[place, :] += rows[k * slab:(k + 1) * slab]


def hidden_kernel(dims, index, *refs):
    peers, blocks, picks, users, per_piece, slab = dims
    grads, pos_grad, target = refs[:3]
    pieces = refs[3:3 + users]
    outs = refs[3 + users:3 + users + peers]
    table, sems = refs[3 + users + peers:]
    stride = per_piece * slab + HEAD
    step = pl.program_id(0)

    @pl.when(step == 0)
    def _():
        load_pieces(pieces, table, sems, stride)

    for r in range(peers):
        first = (r * blocks + step) * picks
        candidates = jnp.concatenate(gather_slabs(table, index, first, picks, per_piece, stride, slab), axis=0)
        result = lax.dot_general(grads[0, r], candidates, TN, preferred_element_type=jnp.float32)
        if r == 0:
            row = jnp.broadcast_to(pos_grad[pl.ds(step, 1), :], (PB, PB)).T
            wide = target[...].astype(jnp.float32)
            for k in range(wide.shape[1] // PB):
                lanes = slice(k * PB, (k + 1) * PB)
                outs[0][:, lanes] = result[:, lanes] + row * wide[:, lanes]
        else:
            outs[r][...] = result


def per_device(hidden, target, pool_table, pool_items, labels, chosen, offsets):
    users, peers = lax.axis_size("users"), lax.axis_size("seq")
    user, peer = lax.axis_index("users"), lax.axis_index("seq")
    length, features = hidden.shape[1], hidden.shape[2]
    blocks, picks = length // PB, chosen.shape[2]
    per_piece = pool_table.shape[0] // NB
    slab = NB // peers
    rows = per_piece * slab
    stride = rows + HEAD
    wide = picks * slab
    factor = 1.0 / (users * (offsets.shape[1] - 1))
    f32, bf16 = jnp.float32, jnp.bfloat16
    params = pltpu.CompilerParams(vmem_limit_bytes=VMEM, dimension_semantics=("arbitrary",))

    narrow = hidden[0].astype(bf16)
    largest = jnp.max(jnp.abs(narrow))

    own_rows = lax.dynamic_slice_in_dim(pool_table.reshape(per_piece, NB, features), peer * slab, slab, axis=1)
    own_ids = lax.dynamic_slice_in_dim(pool_items.reshape(per_piece, NB), peer * slab, slab, axis=1).reshape(1, rows)
    own_ids = jnp.pad(own_ids, ((0, 0), (0, features - rows)))
    head = jnp.concatenate([
        (own_ids // ID_BASE).astype(bf16),
        (own_ids % ID_BASE).astype(bf16),
        jnp.broadcast_to(largest, (1, features)),
        jnp.zeros((HEAD - 3, features), bf16),
    ])
    piece = jnp.concatenate([own_rows.reshape(rows, features), head])

    pieces = {0: piece}
    for q in range(2, users, 2):
        pieces[q] = swap(piece, "users", q)
    for q in range(0, users, 2):
        pieces[q + 1] = swap(pieces[q], "users", 1)
    pieces = [pieces[q] for q in range(users)]

    narrows = {0: narrow, 1: swap(narrow, "seq", 1)}
    for q in range(2, peers, 2):
        narrows[q] = swap(narrow, "seq", q)
        narrows[q + 1] = swap(narrows[q], "seq", 1)
    narrows = [narrows[q] for q in range(peers)]

    spare = -(blocks * picks) % PB
    notes = jnp.concatenate([labels.reshape(-1), jnp.pad(chosen.reshape(-1), (0, spare))]).reshape(-1, PB)
    notes = jnp.stack([notes] + [swap(notes, "seq", q) for q in range(1, peers)])
    label_rows = notes[:, :blocks].astype(f32).transpose(1, 0, 2)
    picked = notes[:, blocks:].reshape(peers, -1)[:, :blocks * picks]
    index = (((picked // per_piece) ^ user) * per_piece + picked % per_piece).reshape(-1)

    owners = peer ^ jnp.arange(peers, dtype=jnp.int32)
    positions = owners[:, None] * length + jnp.arange(length, dtype=jnp.int32)[None, :]
    weights = history_weights(offsets[0], positions).reshape(peers, blocks, PB)

    dims = (peers, blocks, picks, users, per_piece, slab)
    by_block = pl.BlockSpec((PB, features), lambda i, _: (i, 0))
    whole = lambda *shape: pl.BlockSpec(shape, lambda i, _: (0,) * len(shape))
    score_block = pl.BlockSpec((1, peers, wide, PB), lambda i, _: (i, 0, 0, 0))
    anywhere = pl.BlockSpec(memory_space=pl.ANY)
    stat_rows = 2 * peers * blocks + 8
    work = 2 * peers * length * wide * features

    scores, stats, positives = pl.pallas_call(
        functools.partial(score_kernel, dims),
        grid_spec=pltpu.PrefetchScalarGridSpec(
            num_scalar_prefetch=1,
            grid=(blocks,),
            in_specs=[pl.BlockSpec((1, peers, PB), lambda i, _: (i, 0, 0))] + [by_block] * (peers + 1) + [anywhere] * users,
            out_specs=[score_block, whole(stat_rows, PB), whole(blocks, PB)],
            scratch_shapes=[
                pltpu.VMEM((users * stride, features), bf16),
                pltpu.VMEM((users * stride, PB), f32),
                pltpu.SemaphoreType.DMA((users,)),
            ],
        ),
        out_shape=[
            jax.ShapeDtypeStruct((blocks, peers, wide, PB), f32),
            jax.ShapeDtypeStruct((stat_rows, PB), f32),
            jax.ShapeDtypeStruct((blocks, PB), f32),
        ],
        compiler_params=params,
        cost_estimate=pl.CostEstimate(flops=work, bytes_accessed=16 << 20, transcendentals=0),
        name="scores",
    )(index, label_rows, *narrows, target[0], *pieces)

    all_stats = [stats] + [swap(stats, "seq", q) for q in range(1, peers)]

    grads, partial, pos_grad, losses, bound = pl.pallas_call(
        functools.partial(table_kernel, dims + (factor,)),
        grid_spec=pltpu.PrefetchScalarGridSpec(
            num_scalar_prefetch=1,
            grid=(blocks,),
            in_specs=[score_block, whole(peers, blocks, PB), whole(blocks, PB)]
            + [whole(stat_rows, PB)] * peers + [by_block] * peers,
            out_specs=[score_block, whole(users * rows, features), whole(blocks, PB), whole(blocks, PB), whole(8, PB)],
            scratch_shapes=[pltpu.VMEM((peers * blocks, PB), f32), pltpu.VMEM((peers * blocks, PB), f32)],
        ),
        out_shape=[
            jax.ShapeDtypeStruct((blocks, peers, wide, PB), bf16),
            jax.ShapeDtypeStruct((users * rows, features), f32),
            jax.ShapeDtypeStruct((blocks, PB), f32),
            jax.ShapeDtypeStruct((blocks, PB), f32),
            jax.ShapeDtypeStruct((8, PB), f32),
        ],
        compiler_params=params,
        cost_estimate=pl.CostEstimate(flops=work, bytes_accessed=20 << 20, transcendentals=0),
        name="table_grads",
    )(index, scores, weights, positives, *all_stats, *narrows)

    ceiling = jnp.maximum(bound[0, 0], 1e-30)
    scale, back = 16384.0 / ceiling, ceiling / 16384.0
    parts = partial.reshape(users, rows, features)
    sums = {}
    for q in reversed(range(0, users, 2)):
        arrived = swap((parts[q + 1] * scale).astype(jnp.float16), "users", 1)
        sums[q] = parts[q] * scale + arrived.astype(f32)
    owned = sums[0]
    for q in reversed(range(2, users, 2)):
        owned = owned + swap(sums[q].astype(jnp.float16), "users", q).astype(f32)

    hiddens = pl.pallas_call(
        functools.partial(hidden_kernel, dims),
        grid_spec=pltpu.PrefetchScalarGridSpec(
            num_scalar_prefetch=1,
            grid=(blocks,),
            in_specs=[score_block, whole(blocks, PB), by_block] + [anywhere] * users,
            out_specs=[by_block] * peers,
            scratch_shapes=[pltpu.VMEM((users * stride, features), bf16), pltpu.SemaphoreType.DMA((users,))],
        ),
        out_shape=[jax.ShapeDtypeStruct((length, features), f32)] * peers,
        compiler_params=params,
        cost_estimate=pl.CostEstimate(flops=work, bytes_accessed=16 << 20, transcendentals=0),
        name="hidden_grads",
    )(index, grads, pos_grad, target[0], *pieces)

    hidden_scale = 16384.0 / factor
    grad_hidden = hiddens[0] + swap(hiddens[1], "seq", 1)
    for q in range(2, peers, 2):
        both = hiddens[q] + swap(hiddens[q + 1], "seq", 1)
        arrived = swap((both * hidden_scale).astype(jnp.float16), "seq", q)
        grad_hidden = grad_hidden + arrived.astype(f32) * (1.0 / hidden_scale)

    total = jnp.broadcast_to(jnp.sum(losses) * factor, (8, PB))
    for axis, size in (("seq", peers), ("users", users)):
        mask = 1
        while mask < size:
            total = total + swap(total, axis, mask)
            mask *= 2
    loss = total[0, 0]

    quarters = {0: owned, 1: swap(owned, "seq", 1)}
    for q in range(2, peers, 2):
        coded = swap(owned.astype(jnp.float16), "seq", q)
        quarters[q], quarters[q + 1] = coded.astype(f32), swap(coded, "seq", 1).astype(f32)
    quarters = jnp.stack([quarters[q] for q in range(peers)]) * back
    ordered = jnp.take(quarters, owners, axis=0).reshape(peers, per_piece, slab, features)
    grad_table = ordered.transpose(1, 0, 2, 3).reshape(pool_table.shape)
    return loss, grad_hidden[None], grad_table


def solution(mesh):
    return jax.shard_map(
        per_device,
        mesh=mesh,
        in_specs=(
            P("users", "seq", None),
            P("users", "seq", None),
            P("users", None),
            P("users"),
            P("users", "seq"),
            P("users", "seq", None),
            P("users", None),
        ),
        out_specs=(P(), P("users", "seq", None), P("users", None)),
        check_vma=False,
    )
```

```python
import functools
import jax
import jax.numpy as jnp
from jax import lax
from jax.experimental import pallas as pl
from jax.experimental.pallas import tpu as pltpu
from jax.sharding import PartitionSpec as P

NB = 256
PB = 128
HEAD = 16
ID_BASE = 128
VMEM = 8 * 1024 * 1024
NT = (((1,), (1,)), ((), ()))
TN = (((0,), (0,)), ((), ()))


def swap(array, axis, mask):
    count = lax.axis_size(axis)
    return lax.ppermute(array, axis, [(i, i ^ mask) for i in range(count)])


def history_weights(bounds, positions):
    starts = bounds[:-1]
    finish = bounds[1:]
    lengths = (finish - starts).astype(jnp.float32)
    inside = (positions[..., None] >= starts) & (positions[..., None] < finish)
    return jnp.sum(jnp.where(inside, 1.0 / lengths, 0.0), axis=-1)


def gather_slabs(table, index, first, count, per_piece, stride, slab):
    rows = []
    for k in range(count):
        base = index[first + k]
        row = (base // per_piece) * stride + (base % per_piece) * slab
        rows.append(table[pl.ds(pl.multiple_of(row, 16), slab), :])
    return jnp.concatenate(rows, axis=0)


def block_of(ref, step):
    return ref[pl.ds(pl.multiple_of(step * PB, PB), PB), :]


def lane_row(columns):
    folded = columns[:, :PB]
    for k in range(1, columns.shape[1] // PB):
        folded = folded + columns[:, k * PB:(k + 1) * PB]
    return jnp.sum(folded.T, axis=0, keepdims=True)


def score_kernel(dims, index, *refs):
    peers, blocks, picks, users, per_piece, slab = dims
    labels, top, narrows = refs[0], refs[1], refs[2:2 + peers]
    target_from, pieces = refs[2 + peers], refs[3 + peers:-7]
    scores, stats, table, items, target, sems, target_sem = refs[-7:]
    rows = per_piece * slab
    stride = rows + HEAD
    kept = 2 * peers * blocks

    copies = [pltpu.make_async_copy(target_from, target, target_sem)]
    for k, piece in enumerate(pieces):
        copies.append(pltpu.make_async_copy(piece, table.at[pl.ds(k * stride, stride)], sems.at[k]))
    for copy in copies:
        copy.start()
    place = lax.broadcasted_iota(jnp.int32, (HEAD, PB), 0)
    units = jnp.where(place == 0, float(ID_BASE), jnp.where(place == 1, 1.0, 0.0)).astype(jnp.bfloat16)
    stats[pl.ds(kept + blocks, 8), :] = top[...]
    for copy in copies:
        copy.wait()
    for k in range(users):
        items[k * stride:k * stride + rows, :] = lax.dot_general(
            table[k * stride + rows:(k + 1) * stride, :rows], units, TN, preferred_element_type=jnp.float32
        )

    def advance(step, _):
        for r in range(peers):
            first = (r * blocks + step) * picks
            narrow = block_of(narrows[r], step)
            candidates = gather_slabs(table, index, first, picks, per_piece, stride, slab)
            ids = gather_slabs(items, index, first, picks, per_piece, stride, slab)
            score = lax.dot_general(candidates, narrow, NT, preferred_element_type=jnp.float32)
            masked = jnp.where(ids == labels[pl.ds(r * blocks + step, 1), :], -1e30, score)
            scores[step, r] = masked
            peak = jnp.max(masked, axis=0, keepdims=True)
            total = jnp.sum(jnp.exp(masked - peak), axis=0, keepdims=True)
            if r == 0:
                positive = lane_row(narrow.astype(jnp.float32) * block_of(target, step).astype(jnp.float32))
                stats[pl.ds(kept + step, 1), :] = positive
                higher = jnp.maximum(peak, positive)
                total = total * jnp.exp(peak - higher) + jnp.exp(positive - higher)
                peak = higher
            stats[pl.ds(r * blocks + step, 1), :] = peak
            stats[pl.ds((peers + r) * blocks + step, 1), :] = total
        return 0

    lax.fori_loop(0, blocks, advance, 0)


def tree_sum(terms):
    while len(terms) > 1:
        terms = [terms[k] + terms[k + 1] for k in range(0, len(terms), 2)]
    return terms[0]


def grad_kernel(dims, index, *refs):
    peers, blocks, picks, users, per_piece, slab, factor = dims
    scores, weights, table = refs[:3]
    stats = refs[3:3 + peers]
    outs = refs[3 + peers:]
    near, far, pos_grad, loss, bound = outs[:5]
    hiddens, (peaks, ratios) = outs[5:4 + peers], outs[4 + peers:]
    kept = 2 * peers * blocks
    stride = per_piece * slab + HEAD

    terms = []
    for r in range(peers):
        tops = [stats[q][pl.ds((q ^ r) * blocks, blocks), :] for q in range(peers)]
        sums = [stats[q][pl.ds((peers + (q ^ r)) * blocks, blocks), :] for q in range(peers)]
        peak = functools.reduce(jnp.maximum, tops)
        total = tree_sum([s * jnp.exp(t - peak) for t, s in zip(tops, sums)])
        weight = weights[r * blocks:(r + 1) * blocks, :]
        peaks[r * blocks:(r + 1) * blocks, :] = peak
        ratios[r * blocks:(r + 1) * blocks, :] = weight * factor / total
        positive = stats[r][pl.ds(kept, blocks), :]
        terms.append(weight * (peak + jnp.log(total) - positive))
        if r == 0:
            pos_grad[...] = weight * factor * (jnp.exp(positive - peak) / total - 1.0)
    loss[...] = jnp.broadcast_to(jnp.sum(tree_sum(terms), keepdims=True) * factor, loss.shape)
    bound[...] = functools.reduce(jnp.maximum, [s[pl.ds(kept + blocks, 8), :] for s in stats])

    def advance(step, _):
        span = pl.ds(pl.multiple_of(step * PB, PB), PB)
        for r in range(peers):
            peak = peaks[pl.ds(r * blocks + step, 1), :]
            ratio = ratios[pl.ds(r * blocks + step, 1), :]
            grad = (jnp.exp(scores[step, r] - peak) * ratio).astype(jnp.bfloat16)
            if r == 0:
                near[step] = grad
            else:
                far[step, r - 1] = grad
                first = (r * blocks + step) * picks
                candidates = gather_slabs(table, index, first, picks, per_piece, stride, slab)
                hiddens[r - 1][span, :] = lax.dot_general(grad, candidates, TN, preferred_element_type=jnp.float32)
        return 0

    lax.fori_loop(0, blocks, advance, 0)


def table_kernel(dims, index, *refs):
    peers, blocks, picks, users, per_piece, slab = dims
    near, far = refs[:2]
    narrows = refs[2:2 + peers]
    partial = refs[2 + peers]
    partial[...] = jnp.zeros_like(partial)

    def advance(step, _):
        for r in range(peers):
            grad = near[step] if r == 0 else far[step, r - 1]
            rows = jnp.dot(grad, block_of(narrows[r], step), preferred_element_type=jnp.float32)
            first = (r * blocks + step) * picks
            for k in range(picks):
                place = pl.ds(pl.multiple_of(index[first + k] * slab, 16), slab)
                partial[place, :] += rows[k * slab:(k + 1) * slab]
        return 0

    lax.fori_loop(0, blocks, advance, 0)


def hidden_kernel(dims, index, near, table, pos_grad, target, out):
    peers, blocks, picks, users, per_piece, slab = dims
    stride = per_piece * slab + HEAD

    def advance(step, _):
        span = pl.ds(pl.multiple_of(step * PB, PB), PB)
        candidates = gather_slabs(table, index, step * picks, picks, per_piece, stride, slab)
        result = lax.dot_general(near[step], candidates, TN, preferred_element_type=jnp.float32)
        row = jnp.broadcast_to(pos_grad[pl.ds(step, 1), :], (PB, PB)).T
        wide = block_of(target, step).astype(jnp.float32)
        for k in range(0, wide.shape[1], PB):
            out[span, k:k + PB] = result[:, k:k + PB] + row * wide[:, k:k + PB]
        return 0

    lax.fori_loop(0, blocks, advance, 0)


def per_device(hidden, target, pool_table, pool_items, labels, chosen, offsets):
    users, peers = lax.axis_size("users"), lax.axis_size("seq")
    user, peer = lax.axis_index("users"), lax.axis_index("seq")
    length, features = hidden.shape[1], hidden.shape[2]
    blocks, picks = length // PB, chosen.shape[2]
    per_piece = pool_table.shape[0] // NB
    slab = NB // peers
    rows = per_piece * slab
    stride = rows + HEAD
    wide = picks * slab
    factor = 1.0 / (users * (offsets.shape[1] - 1))
    f32, bf16 = jnp.float32, jnp.bfloat16

    narrow = hidden[0].astype(bf16)
    largest = jnp.max(jnp.abs(narrow))

    def halves(whole_numbers):
        numbers = whole_numbers.reshape(-1)
        numbers = jnp.pad(numbers, (0, -numbers.shape[0] % features)).reshape(-1, features)
        return [(numbers // ID_BASE).astype(bf16), (numbers % ID_BASE).astype(bf16)]

    def whole_again(array, row, count):
        lines = -(-count // features)
        high, low = array[row:row + lines], array[row + lines:row + 2 * lines]
        return (high.astype(f32) * ID_BASE + low.astype(f32)).reshape(-1)[:count], row + 2 * lines

    own_rows = lax.dynamic_slice_in_dim(pool_table.reshape(per_piece, NB, features), peer * slab, slab, axis=1)
    own_ids = lax.dynamic_slice_in_dim(pool_items.reshape(per_piece, NB), peer * slab, slab, axis=1)
    spare = jnp.zeros((HEAD - 2, features), bf16)
    piece = jnp.concatenate([own_rows.reshape(rows, features)] + halves(own_ids) + [spare])

    notes = jnp.concatenate(halves(labels) + halves(chosen))
    notes = jnp.pad(notes, ((0, -notes.shape[0] % 16), (0, 0)))
    packed = jnp.concatenate([narrow, notes])
    top = jnp.broadcast_to(largest.astype(f32), (8, PB))

    pairs = users // 2
    batches = [[pairs - 1] + list(range(1, pairs // 2)), list(range(pairs // 2, pairs - 1))]
    pieces = {0: piece, 1: swap(piece, "users", 1)}
    states = {0: packed}
    for q in range(2, peers, 2):
        states[q] = swap(packed, "seq", q)
    top = jnp.maximum(top, swap(top, "users", 1))
    held = piece
    for turn, batch in enumerate(batches):
        came = [swap(held, "users", 2 * k) for k in batch]
        came, top, pieces, held = lax.optimization_barrier((came, top, pieces, piece))
        for k, part in zip(batch, came):
            pieces[2 * k] = part
            pieces[2 * k + 1] = swap(part, "users", 1)
        top = jnp.maximum(top, swap(top, "users", 2 << turn))
    mask = 2 << len(batches)
    while mask < users:
        top = jnp.maximum(top, swap(top, "users", mask))
        mask *= 2
    own, _ = lax.optimization_barrier((packed, came))
    states[1] = swap(own, "seq", 1)
    for q in range(2, peers, 2):
        states[q + 1] = swap(states[q], "seq", 1)
    narrows = [states[q] for q in range(peers)]
    pieces = [pieces[q] for q in range(users)]

    label_rows, picked = [], []
    for state in narrows:
        line, row = whole_again(state, length, length)
        label_rows.append(line.reshape(blocks, PB))
        line, row = whole_again(state, row, blocks * picks)
        picked.append(line.astype(jnp.int32))
    label_rows, picked = jnp.concatenate(label_rows), jnp.concatenate(picked)
    owner = picked // per_piece
    index = (owner ^ user) * per_piece + picked % per_piece

    owners = peer ^ jnp.arange(peers, dtype=jnp.int32)
    positions = owners[:, None] * length + jnp.arange(length, dtype=jnp.int32)[None, :]
    weights = history_weights(offsets[0], positions).reshape(peers * blocks, PB)
    weights, label_rows, index, top = lax.optimization_barrier((weights, label_rows, index, top))

    dims = (peers, blocks, picks, users, per_piece, slab)
    half = features // 2
    stat_rows = (2 * peers + 1) * blocks + 8
    in_vmem, in_smem = pl.BlockSpec(memory_space=pltpu.VMEM), pl.BlockSpec(memory_space=pltpu.SMEM)
    in_hbm = pl.BlockSpec(memory_space=pltpu.HBM)
    cost = pl.CostEstimate(flops=1 << 20, bytes_accessed=1 << 20, transcendentals=0)
    params = pltpu.CompilerParams(vmem_limit_bytes=VMEM)

    def call(kernel, name, outs, scratch, rows_of, *operands, unplaced=0):
        placed = len(operands) - unplaced
        return pl.pallas_call(
            kernel,
            in_specs=[in_smem] + [in_vmem] * placed + [in_hbm] * unplaced,
            out_specs=[in_vmem] * len(outs),
            out_shape=[jax.ShapeDtypeStruct(shape, dtype) for shape, dtype in outs],
            scratch_shapes=scratch,
            compiler_params=params, cost_estimate=cost, name=name,
        )(rows_of, *operands[:placed], *[pltpu.with_memory_space_constraint(x, pltpu.HBM) for x in operands[placed:]])

    scores, stats, table = call(
        functools.partial(score_kernel, dims), "scores",
        [((blocks, peers, wide, PB), f32), ((stat_rows, PB), f32), ((users * stride, features), bf16)],
        [
            pltpu.VMEM((users * stride, PB), f32),
            pltpu.VMEM((length, features), bf16),
            pltpu.SemaphoreType.DMA((users,)),
            pltpu.SemaphoreType.DMA,
        ],
        index, label_rows, top, *narrows, target[0], *pieces, unplaced=1 + users,
    )
    all_stats = [stats] + [swap(stats, "seq", q) for q in range(1, peers)]

    state_out = ((length, features), f32)
    near, far, pos_grad, loss, bound, *hiddens = call(
        functools.partial(grad_kernel, dims + (factor,)), "grads",
        [
            ((blocks, wide, PB), bf16),
            ((blocks, peers - 1, wide, PB), bf16),
            ((blocks, PB), f32),
            ((8, PB), f32),
            ((8, PB), f32),
        ] + [state_out] * (peers - 1),
        [pltpu.VMEM((peers * blocks, PB), f32)] * 2,
        index, scores, weights, table, *all_stats,
    )
    from_core = [swap(hiddens[q], "seq", 1) for q in range(2, peers, 2)]
    loss_arrived = swap(loss, "users", 1)
    (partial,) = call(
        functools.partial(table_kernel, dims), "table_grads", [((users * rows, features), f32)], [],
        index, near, far, *narrows,
    )
    partial, from_core, loss_arrived = lax.optimization_barrier((partial, from_core, loss_arrived))

    ceiling = jnp.maximum(bound[0, 0], 1e-30)
    scale, back = 16384.0 / ceiling, ceiling / 16384.0

    parts = partial.reshape(pairs, 2, rows, features)
    halved = [slice(0, half), slice(half, features)]

    def with_partner(lanes, arrived):
        sums = parts[:, 0, :, lanes] * scale + arrived.astype(f32)
        return sums[0], sums.astype(jnp.float16)

    def with_owners(owned, sent):
        for k in reversed(range(1, pairs)):
            owned = owned + swap(sent[k], "users", 2 * k).astype(f32)
        return owned

    hidden_scale = 16384.0 / factor
    hidden_coded = [
        [((hiddens[2 * k + 1][:, lanes] + part[:, lanes]) * hidden_scale).astype(jnp.float16) for lanes in halved]
        for k, part in enumerate(from_core)
    ]
    first_coded, second_coded = [(parts[:, 1, :, lanes] * scale).astype(jnp.float16) for lanes in halved]
    first_coded, hidden_coded = lax.optimization_barrier((first_coded, hidden_coded))
    hidden_arrived = [[swap(two[0], "seq", 2 * k + 2)] for k, two in enumerate(hidden_coded)]
    first_arrived = swap(first_coded, "users", 1)
    own_core = swap(hiddens[0], "seq", 1)
    loss = loss + loss_arrived
    mask = 2
    while mask < users:
        loss = loss + swap(loss, "users", mask)
        mask *= 2
    first_arrived, loss, second_coded, hidden_arrived, own_core, hidden_coded = lax.optimization_barrier(
        (first_arrived, loss, second_coded, hidden_arrived, own_core, hidden_coded)
    )
    second_arrived = swap(second_coded, "users", 1)
    for k, two in enumerate(hidden_coded):
        hidden_arrived[k].append(swap(two[1], "seq", 2 * k + 2))
    owned_first, sent_first = with_partner(halved[0], first_arrived)
    owned_first = with_owners(owned_first, sent_first)
    owned_first, second_arrived, near, hidden_arrived = lax.optimization_barrier(
        (owned_first, second_arrived, near, hidden_arrived)
    )
    owned_second, sent_second = with_partner(halved[1], second_arrived)
    owned_second = with_owners(owned_second, sent_second)
    (own_hidden,) = call(
        functools.partial(hidden_kernel, dims), "own_hidden_grads", [state_out], [],
        index, near, table, pos_grad, target[0],
    )
    grad_hidden = own_hidden + own_core
    for two in hidden_arrived:
        grad_hidden = grad_hidden + jnp.concatenate(two, axis=1).astype(f32) * (1.0 / hidden_scale)
    owned = jnp.concatenate([owned_first, owned_second], axis=1)
    loss = loss[0, 0]

    quarters = {0: owned, 1: swap(owned, "seq", 1)}
    for q in range(2, peers, 2):
        coded = swap(owned.astype(jnp.float16), "seq", q)
        quarters[q], quarters[q + 1] = coded.astype(f32), swap(coded, "seq", 1).astype(f32)
    grad_table = jnp.zeros((per_piece, peers, slab, features), f32)
    for q in range(peers):
        quarter = (quarters[q] * back).reshape(per_piece, 1, slab, features)
        grad_table = lax.dynamic_update_slice_in_dim(grad_table, quarter, peer ^ q, axis=1)
    return loss, grad_hidden[None], grad_table.reshape(pool_table.shape)


def solution(mesh):
    return jax.shard_map(
        per_device,
        mesh=mesh,
        in_specs=(
            P("users", "seq", None),
            P("users", "seq", None),
            P("users", None),
            P("users"),
            P("users", "seq"),
            P("users", "seq", None),
            P("users", None),
        ),
        out_specs=(P(), P("users", "seq", None), P("users", None)),
        check_vma=False,
    )
```

```python
import functools
import jax
import jax.numpy as jnp
from jax import lax
from jax.experimental import pallas as pl
from jax.experimental.pallas import tpu as pltpu
from jax.sharding import PartitionSpec as P

NB = 256
PB = 128
HEAD = 16
ID_BASE = 128
VMEM = 8 * 1024 * 1024
NT = (((1,), (1,)), ((), ()))
TN = (((0,), (0,)), ((), ()))


def swap(array, axis, mask):
    count = lax.axis_size(axis)
    return lax.ppermute(array, axis, [(i, i ^ mask) for i in range(count)])


def history_weights(bounds, positions):
    starts = bounds[:-1]
    finish = bounds[1:]
    lengths = (finish - starts).astype(jnp.float32)
    inside = (positions[..., None] >= starts) & (positions[..., None] < finish)
    return jnp.sum(jnp.where(inside, 1.0 / lengths, 0.0), axis=-1)


def gather_slabs(table, index, first, count, per_piece, stride, slab):
    rows = []
    for k in range(count):
        base = index[first + k]
        row = (base // per_piece) * stride + (base % per_piece) * slab
        rows.append(table[pl.ds(pl.multiple_of(row, 16), slab), :])
    return jnp.concatenate(rows, axis=0)


def block_of(ref, step):
    return ref[pl.ds(pl.multiple_of(step * PB, PB), PB), :]


def lane_row(columns):
    folded = columns[:, :PB]
    for k in range(1, columns.shape[1] // PB):
        folded = folded + columns[:, k * PB:(k + 1) * PB]
    return jnp.sum(folded.T, axis=0, keepdims=True)


def score_kernel(dims, index, *refs):
    peers, blocks, picks, users, per_piece, slab = dims
    labels, narrows = refs[0], refs[1:1 + peers]
    target_from, pieces = refs[1 + peers], refs[2 + peers:-7]
    scores, stats, table, items, target, sems, target_sem = refs[-7:]
    rows = per_piece * slab
    stride = rows + HEAD
    kept = 2 * peers * blocks

    target_copy = pltpu.make_async_copy(target_from, target, target_sem)
    target_copy.start()
    copies = [
        pltpu.make_async_copy(piece, table.at[pl.ds(k * stride, stride)], sems.at[k])
        for k, piece in enumerate(pieces)
    ]
    for copy in copies:
        copy.start()
    place = lax.broadcasted_iota(jnp.int32, (HEAD, PB), 0)
    units = jnp.where(place == 0, float(ID_BASE), jnp.where(place == 1, 1.0, 0.0)).astype(jnp.bfloat16)
    top = [narrow[narrow.shape[0] - HEAD:, :PB].astype(jnp.float32)[HEAD - 1:] for narrow in narrows]
    stats[pl.ds(kept + blocks, 8), :] = jnp.broadcast_to(functools.reduce(jnp.maximum, top), (8, PB))
    target_copy.wait()
    for copy in copies:
        copy.wait()
    for k in range(users):
        items[k * stride:k * stride + rows, :] = lax.dot_general(
            table[k * stride + rows:(k + 1) * stride, :rows], units, TN, preferred_element_type=jnp.float32
        )

    def advance(step, _):
        for r in range(peers):
            first = (r * blocks + step) * picks
            narrow = block_of(narrows[r], step)
            candidates = gather_slabs(table, index, first, picks, per_piece, stride, slab)
            ids = gather_slabs(items, index, first, picks, per_piece, stride, slab)
            score = lax.dot_general(candidates, narrow, NT, preferred_element_type=jnp.float32)
            masked = jnp.where(ids == labels[pl.ds(r * blocks + step, 1), :], -1e30, score)
            scores[step, r] = masked
            peak = jnp.max(masked, axis=0, keepdims=True)
            total = jnp.sum(jnp.exp(masked - peak), axis=0, keepdims=True)
            if r == 0:
                positive = lane_row(narrow.astype(jnp.float32) * block_of(target, step).astype(jnp.float32))
                stats[pl.ds(kept + step, 1), :] = positive
                higher = jnp.maximum(peak, positive)
                total = total * jnp.exp(peak - higher) + jnp.exp(positive - higher)
                peak = higher
            stats[pl.ds(r * blocks + step, 1), :] = peak
            stats[pl.ds((peers + r) * blocks + step, 1), :] = total
        return 0

    lax.fori_loop(0, blocks, advance, 0)


def tree_sum(terms):
    while len(terms) > 1:
        terms = [terms[k] + terms[k + 1] for k in range(0, len(terms), 2)]
    return terms[0]


def grad_kernel(dims, index, *refs):
    peers, blocks, picks, users, per_piece, slab, factor = dims
    scores, weights, table = refs[:3]
    stats = refs[3:3 + peers]
    outs = refs[3 + peers:]
    near, far, pos_grad, word = outs[:4]
    hiddens, (peaks, ratios) = outs[4:3 + peers], outs[3 + peers:]
    kept = 2 * peers * blocks
    stride = per_piece * slab + HEAD

    terms = []
    for r in range(peers):
        tops = [stats[q][pl.ds((q ^ r) * blocks, blocks), :] for q in range(peers)]
        sums = [stats[q][pl.ds((peers + (q ^ r)) * blocks, blocks), :] for q in range(peers)]
        peak = functools.reduce(jnp.maximum, tops)
        total = tree_sum([s * jnp.exp(t - peak) for t, s in zip(tops, sums)])
        weight = weights[r * blocks:(r + 1) * blocks, :]
        peaks[r * blocks:(r + 1) * blocks, :] = peak
        ratios[r * blocks:(r + 1) * blocks, :] = weight * factor / total
        positive = stats[r][pl.ds(kept, blocks), :]
        terms.append(weight * (peak + jnp.log(total) - positive))
        if r == 0:
            pos_grad[...] = weight * factor * (jnp.exp(positive - peak) / total - 1.0)
    word[:4, :] = jnp.broadcast_to(jnp.sum(tree_sum(terms), keepdims=True) * factor, (4, word.shape[1]))
    top = jnp.maximum(stats[0][pl.ds(kept + blocks, 4), :], 1e-30)
    word[4:, :] = top

    def advance(step, _):
        span = pl.ds(pl.multiple_of(step * PB, PB), PB)
        for r in range(peers):
            peak = peaks[pl.ds(r * blocks + step, 1), :]
            ratio = ratios[pl.ds(r * blocks + step, 1), :]
            grad = (jnp.exp(scores[step, r] - peak) * ratio).astype(jnp.bfloat16)
            if r == 0:
                near[step] = grad
            else:
                far[step, r - 1] = grad
                first = (r * blocks + step) * picks
                candidates = gather_slabs(table, index, first, picks, per_piece, stride, slab)
                hiddens[r - 1][span, :] = lax.dot_general(grad, candidates, TN, preferred_element_type=jnp.float32)
        return 0

    lax.fori_loop(0, blocks, advance, 0)


def table_kernel(dims, index, *refs):
    peers, blocks, picks, users, per_piece, slab = dims
    near, far = refs[:2]
    narrows = refs[2:2 + peers]
    partial = refs[2 + peers]
    partial[...] = jnp.zeros_like(partial)

    def advance(step, _):
        for r in range(peers):
            grad = near[step] if r == 0 else far[step, r - 1]
            rows = jnp.dot(grad, block_of(narrows[r], step), preferred_element_type=jnp.float32)
            first = (r * blocks + step) * picks
            for k in range(picks):
                place = pl.ds(pl.multiple_of(index[first + k] * slab, 16), slab)
                partial[place, :] += rows[k * slab:(k + 1) * slab]
        return 0

    lax.fori_loop(0, blocks, advance, 0)


def hidden_kernel(dims, index, near, table, pos_grad, target, out):
    peers, blocks, picks, users, per_piece, slab = dims
    stride = per_piece * slab + HEAD

    def advance(step, _):
        span = pl.ds(pl.multiple_of(step * PB, PB), PB)
        candidates = gather_slabs(table, index, step * picks, picks, per_piece, stride, slab)
        result = lax.dot_general(near[step], candidates, TN, preferred_element_type=jnp.float32)
        row = jnp.broadcast_to(pos_grad[pl.ds(step, 1), :], (PB, PB)).T
        wide = block_of(target, step).astype(jnp.float32)
        for k in range(0, wide.shape[1], PB):
            out[span, k:k + PB] = result[:, k:k + PB] + row * wide[:, k:k + PB]
        return 0

    lax.fori_loop(0, blocks, advance, 0)


def per_device(hidden, target, pool_table, pool_items, labels, chosen, offsets):
    users, peers = lax.axis_size("users"), lax.axis_size("seq")
    user, peer = lax.axis_index("users"), lax.axis_index("seq")
    length, features = hidden.shape[1], hidden.shape[2]
    blocks, picks = length // PB, chosen.shape[2]
    per_piece = pool_table.shape[0] // NB
    slab = NB // peers
    rows = per_piece * slab
    stride = rows + HEAD
    wide = picks * slab
    factor = 1.0 / (users * (offsets.shape[1] - 1))
    f32, bf16 = jnp.float32, jnp.bfloat16

    narrow = hidden[0].astype(bf16)
    largest = jnp.max(jnp.abs(narrow))

    def halves(whole_numbers):
        numbers = whole_numbers.reshape(-1)
        numbers = jnp.pad(numbers, (0, -numbers.shape[0] % features)).reshape(-1, features)
        return [(numbers // ID_BASE).astype(bf16), (numbers % ID_BASE).astype(bf16)]

    def whole_again(array, row, count):
        lines = -(-count // features)
        high, low = array[row:row + lines], array[row + lines:row + 2 * lines]
        return (high.astype(f32) * ID_BASE + low.astype(f32)).reshape(-1)[:count], row + 2 * lines

    own_rows = lax.dynamic_slice_in_dim(pool_table.reshape(per_piece, NB, features), peer * slab, slab, axis=1)
    own_ids = lax.dynamic_slice_in_dim(pool_items.reshape(per_piece, NB), peer * slab, slab, axis=1)
    spare = jnp.zeros((HEAD - 2, features), bf16)
    piece = jnp.concatenate([own_rows.reshape(rows, features)] + halves(own_ids) + [spare])

    notes = halves(labels) + halves(chosen)
    spare = -(sum(note.shape[0] for note in notes) + 1) % HEAD
    notes += [jnp.zeros((spare, features), bf16), jnp.broadcast_to(largest, (1, features))]
    packed = jnp.concatenate([narrow] + notes)

    pieces = {0: piece, 1: swap(piece, "users", 1)}
    states = {0: packed}
    for q in range(2, peers, 2):
        states[q] = swap(packed, "seq", q)
    pairs = users // 2
    if pairs == 4:
        pieces[4], pieces[2] = swap(piece, "users", 4), swap(piece, "users", 2)
        pieces = lax.optimization_barrier(pieces)
        pieces[6], pieces[5] = swap(pieces[4], "users", 2), swap(pieces[4], "users", 1)
        pieces = lax.optimization_barrier(pieces)
        own, came = lax.optimization_barrier((packed, pieces[6]))
        pieces[7], pieces[3] = swap(pieces[6], "users", 1), swap(pieces[1], "users", 2)
    else:
        for q in range(2, users, 2):
            pieces[q] = swap(piece, "users", q)
            pieces[q + 1] = swap(pieces[q], "users", 1)
        own = packed
    states[1] = swap(own, "seq", 1)
    for q in range(2, peers, 2):
        states[q + 1] = swap(states[q], "seq", 1)
    narrows = [states[q] for q in range(peers)]
    pieces = [pieces[q] for q in range(users)]

    label_rows, picked = [], []
    for state in narrows:
        line, row = whole_again(state, length, length)
        label_rows.append(line.reshape(blocks, PB))
        line, row = whole_again(state, row, blocks * picks)
        picked.append(line.astype(jnp.int32))
    label_rows, picked = jnp.concatenate(label_rows), jnp.concatenate(picked)
    owner = picked // per_piece
    index = (owner ^ user) * per_piece + picked % per_piece

    owners = peer ^ jnp.arange(peers, dtype=jnp.int32)
    positions = owners[:, None] * length + jnp.arange(length, dtype=jnp.int32)[None, :]
    weights = history_weights(offsets[0], positions).reshape(peers * blocks, PB)
    weights, label_rows, index = lax.optimization_barrier((weights, label_rows, index))

    dims = (peers, blocks, picks, users, per_piece, slab)
    half = features // 2
    stat_rows = (2 * peers + 1) * blocks + 8
    in_vmem, in_smem = pl.BlockSpec(memory_space=pltpu.VMEM), pl.BlockSpec(memory_space=pltpu.SMEM)
    in_hbm = pl.BlockSpec(memory_space=pltpu.HBM)
    cost = pl.CostEstimate(flops=1 << 20, bytes_accessed=1 << 20, transcendentals=0)
    params = pltpu.CompilerParams(vmem_limit_bytes=VMEM)

    def call(kernel, name, outs, scratch, rows_of, *operands, unplaced=0):
        placed = len(operands) - unplaced
        return pl.pallas_call(
            kernel,
            in_specs=[in_smem] + [in_vmem] * placed + [in_hbm] * unplaced,
            out_specs=[in_vmem] * len(outs),
            out_shape=[jax.ShapeDtypeStruct(shape, dtype) for shape, dtype in outs],
            scratch_shapes=scratch,
            compiler_params=params, cost_estimate=cost, name=name,
        )(rows_of, *operands[:placed], *[pltpu.with_memory_space_constraint(x, pltpu.HBM) for x in operands[placed:]])

    scores, stats, table = call(
        functools.partial(score_kernel, dims), "scores",
        [((blocks, peers, wide, PB), f32), ((stat_rows, PB), f32), ((users * stride, features), bf16)],
        [
            pltpu.VMEM((users * stride, PB), f32),
            pltpu.VMEM((length, features), bf16),
            pltpu.SemaphoreType.DMA((users,)),
            pltpu.SemaphoreType.DMA,
        ],
        index, label_rows, *narrows, target[0], *pieces, unplaced=1 + users,
    )
    all_stats = [stats] + [swap(stats, "seq", q) for q in range(1, peers)]

    state_out = ((length, features), f32)
    near, far, pos_grad, word, *hiddens = call(
        functools.partial(grad_kernel, dims + (factor,)), "grads",
        [
            ((blocks, wide, PB), bf16),
            ((blocks, peers - 1, wide, PB), bf16),
            ((blocks, PB), f32),
            ((8, PB), f32),
        ] + [state_out] * (peers - 1),
        [pltpu.VMEM((peers * blocks, PB), f32)] * 2,
        index, scores, weights, table, *all_stats,
    )

    def meet(ours, theirs):
        row = lax.broadcasted_iota(jnp.int32, ours.shape, 0)
        return jnp.where(row < 4, ours + theirs, jnp.maximum(ours, theirs))

    from_core = [swap(hiddens[q], "seq", 1) for q in range(2, peers, 2)]
    partner_word = swap(word, "users", 1)
    (partial,) = call(
        functools.partial(table_kernel, dims), "table_grads", [((users * rows, features), f32)], [],
        index, near, far, *narrows,
    )
    partial, from_core, partner_word = lax.optimization_barrier((partial, from_core, partner_word))

    hidden_scale = 16384.0 / factor

    parts = partial.reshape(users, rows, features)
    halved = [slice(0, half), slice(half, features)]

    def coded(sums, bound):
        return (sums * (16384.0 / bound)).astype(jnp.float16)

    def added(sums, *arrived):
        for part, bound in arrived:
            sums = sums + part.astype(f32) * (bound / 16384.0)
        return sums

    def bound_of(word):
        row = jnp.maximum(word[4:5], 1e-30)
        return jnp.concatenate([row] * (features // PB), axis=1)

    def coded_hiddens(lanes):
        return [
            ((hiddens[2 * k + 1][:, lanes] + part[:, lanes]) * hidden_scale).astype(jnp.float16)
            for k, part in enumerate(from_core)
        ]

    def with_far(coded):
        return [swap(part, "seq", 2 * k + 2) for k, part in enumerate(coded)]

    word = meet(word, partner_word)
    if pairs == 4:
        pair_bound = bound_of(word)
        sent, hidden_coded = lax.optimization_barrier(
            ([coded(parts[7], pair_bound), coded(parts[3], pair_bound)], coded_hiddens(halved[0]))
        )
        from_pair, from_line = swap(sent[0], "users", 1), swap(sent[1], "users", 2)
        hidden_arrived = [with_far(hidden_coded)]
        line_word = swap(word, "users", 2)
        own_core = swap(hiddens[0], "seq", 1)
        from_pair, from_line, line_word = lax.optimization_barrier((from_pair, from_line, line_word))
        line_bound, word = bound_of(line_word), meet(word, line_word)
        four_bound = bound_of(word)
        pair_sum = added(parts[1], (from_line, line_bound))
        sent = [coded(added(parts[6], (from_pair, pair_bound)), four_bound), coded(parts[5], four_bound)]

        from_line, from_pair = swap(sent[0], "users", 2), swap(sent[1], "users", 1)
        far_word = swap(word, "users", 4)
        from_pair, from_line, far_word, hidden_arrived, own_core, hidden_coded, near = lax.optimization_barrier(
            (from_pair, from_line, far_word, hidden_arrived, own_core, coded_hiddens(halved[1]), near)
        )
        word = meet(word, far_word)
        top = bound_of(word)
        far_sum = added(parts[4], (from_line, four_bound), (from_pair, four_bound))
        sent = [coded(far_sum, top), coded(parts[2], top), coded(pair_sum, top)]

        arrived = [swap(sent[0], "users", 4), swap(sent[1], "users", 2), swap(sent[2], "users", 1)]
        hidden_arrived.append(with_far(hidden_coded))
        (own_hidden,) = call(
            functools.partial(hidden_kernel, dims), "own_hidden_grads", [state_out], [],
            index, near, table, pos_grad, target[0],
        )
        arrived, own_hidden, hidden_arrived = lax.optimization_barrier((arrived, own_hidden, hidden_arrived))
        owned = added(parts[0], *[(part, top) for part in arrived])
    else:
        mask = 2
        while mask < users:
            word = meet(word, swap(word, "users", mask))
            mask *= 2
        top = bound_of(word)
        owned = parts[0]
        for q in range(0, users, 2):
            sums = added(parts[q], (swap(coded(parts[q + 1], top), "users", 1), top))
            owned = sums if q == 0 else added(owned, (swap(coded(sums, top), "users", q), top))
        hidden_arrived = [with_far(coded_hiddens(lanes)) for lanes in halved]
        own_core = swap(hiddens[0], "seq", 1)
        (own_hidden,) = call(
            functools.partial(hidden_kernel, dims), "own_hidden_grads", [state_out], [],
            index, near, table, pos_grad, target[0],
        )

    quarters = {0: owned, 1: swap(owned, "seq", 1)}
    for q in range(2, peers, 2):
        coded_owned = swap(coded(owned, top), "seq", q)
        quarters[q] = added(0.0, (coded_owned, top))
        quarters[q + 1] = added(0.0, (swap(coded_owned, "seq", 1), top))
    grad_hidden = own_hidden + own_core
    for k in range(peers // 2 - 1):
        part = jnp.concatenate([lanes[k] for lanes in hidden_arrived], axis=1)
        grad_hidden = grad_hidden + part.astype(f32) * (1.0 / hidden_scale)
    grad_table = jnp.zeros((per_piece, peers, slab, features), f32)
    for q in range(peers):
        quarter = quarters[q].reshape(per_piece, 1, slab, features)
        grad_table = lax.dynamic_update_slice_in_dim(grad_table, quarter, peer ^ q, axis=1)
    return word[0, 0], grad_hidden[None], grad_table.reshape(pool_table.shape)


def solution(mesh):
    return jax.shard_map(
        per_device,
        mesh=mesh,
        in_specs=(
            P("users", "seq", None),
            P("users", "seq", None),
            P("users", None),
            P("users"),
            P("users", "seq"),
            P("users", "seq", None),
            P("users", None),
        ),
        out_specs=(P(), P("users", "seq", None), P("users", None)),
        check_vma=False,
    )
```

```python
import functools
import jax
import jax.numpy as jnp
from jax import lax
from jax.experimental import pallas as pl
from jax.experimental.pallas import tpu as pltpu
from jax.sharding import PartitionSpec as P

NB = 256
PB = 128
HEAD = 16
ID_BASE = 128
VMEM = 8 * 1024 * 1024
NT = (((1,), (1,)), ((), ()))
TN = (((0,), (0,)), ((), ()))


def swap(array, axis, mask):
    count = lax.axis_size(axis)
    return lax.ppermute(array, axis, [(i, i ^ mask) for i in range(count)])


def history_weights(bounds, positions):
    starts = bounds[:-1]
    finish = bounds[1:]
    lengths = (finish - starts).astype(jnp.float32)
    inside = (positions[..., None] >= starts) & (positions[..., None] < finish)
    return jnp.sum(jnp.where(inside, 1.0 / lengths, 0.0), axis=-1)


def note_places(length, features, blocks):
    lines = length // features
    return lines, 2 * lines, -(-(2 * lines + blocks + 1) // HEAD) * HEAD


def gather_slabs(table, bases, per_piece, stride, slab):
    rows = []
    for base in bases:
        row = (base // per_piece) * stride + (base % per_piece) * slab
        rows.append(table[pl.ds(pl.multiple_of(row, 16), slab), :])
    return jnp.concatenate(rows, axis=0)


def block_of(ref, step):
    return ref[pl.ds(pl.multiple_of(step * PB, PB), PB), :]


def lane_row(columns):
    folded = columns[:, :PB]
    for k in range(1, columns.shape[1] // PB):
        folded = folded + columns[:, k * PB:(k + 1) * PB]
    return jnp.sum(folded.T, axis=0, keepdims=True)


def pack_kernel(labels_from, chosen_from, hidden_from, packed, labels, chosen, hidden, lots, sems, note_sems):
    note_copies = [
        pltpu.make_async_copy(labels_from, labels, note_sems.at[0]),
        pltpu.make_async_copy(chosen_from, chosen, note_sems.at[1]),
    ]
    for copy in note_copies:
        copy.start()
    length, features = hidden.shape
    blocks, picks = chosen.shape
    lines, first, count = note_places(length, features, blocks)
    part = length // sems.shape[0]
    copies = [
        pltpu.make_async_copy(hidden_from.at[pl.ds(k * part, part)], hidden.at[pl.ds(k * part, part)], sems.at[k])
        for k in range(sems.shape[0])
    ]
    for copy in copies:
        copy.start()
    lots[...] = jnp.zeros_like(lots)
    for copy in note_copies:
        copy.wait()
    lots[:, :picks] = chosen[...].astype(jnp.float32)
    row = lax.broadcasted_iota(jnp.int32, (count, features), 0)
    notes = jnp.zeros((count, features), jnp.float32)
    for k in range(lines):
        line = labels[:, k * features:(k + 1) * features]
        notes = jnp.where(row == k, (line // ID_BASE).astype(jnp.float32), notes)
        notes = jnp.where(row == lines + k, (line % ID_BASE).astype(jnp.float32), notes)
    for k in range(blocks):
        notes = jnp.where(row == first + k, lots[k:k + 1, :], notes)
    top = jnp.zeros((8, features), jnp.float32)
    for k, copy in enumerate(copies):
        copy.wait()
        narrow = hidden[k * part:(k + 1) * part, :].astype(jnp.bfloat16)
        packed[k * part:(k + 1) * part, :] = narrow
        sizes = jnp.abs(narrow.astype(jnp.float32))
        top = jnp.maximum(top, jnp.max(sizes.reshape(part // 8, 8, features), axis=0))
    notes = jnp.where(row == count - 1, jnp.max(top, keepdims=True), notes)
    packed[length:, :] = notes.astype(jnp.bfloat16)


def score_kernel(dims, user, *refs):
    peers, blocks, picks, users, per_piece, slab = dims
    narrows, target_from, pieces = refs[:peers], refs[peers], refs[1 + peers:-11]
    scores, stats, table, index, items, target, labels, lots, sems, target_sem, index_sem = refs[-11:]
    rows = per_piece * slab
    stride = rows + HEAD
    kept = 2 * peers * blocks
    length, features = target.shape
    lines, first_lot, _ = note_places(length, features, blocks)

    target_copy = pltpu.make_async_copy(target_from, target, target_sem)
    target_copy.start()
    copies = [
        pltpu.make_async_copy(piece, table.at[pl.ds(k * stride, stride)], sems.at[k])
        for k, piece in enumerate(pieces)
    ]
    for copy in copies:
        copy.start()
    tops = []
    for r in range(peers):
        notes = narrows[r][length:, :].astype(jnp.float32)
        lot = notes[first_lot:first_lot + blocks, :PB].astype(jnp.int32)
        lots[r * blocks:(r + 1) * blocks, :] = ((lot // per_piece) ^ user[0]) * per_piece + lot % per_piece
        for k in range(blocks):
            line, lane = divmod(k * PB, features)
            high, low = notes[line:line + 1, lane:lane + PB], notes[lines + line:lines + line + 1, lane:lane + PB]
            labels[r * blocks + k:r * blocks + k + 1, :] = high * ID_BASE + low
        tops.append(notes[-1:, :PB])
    index_copy = pltpu.make_async_copy(lots, index, index_sem)
    index_copy.start()
    stats[pl.ds(kept + blocks, 8), :] = jnp.broadcast_to(functools.reduce(jnp.maximum, tops), (8, PB))
    place = lax.broadcasted_iota(jnp.int32, (HEAD, PB), 0)
    units = jnp.where(place == 0, float(ID_BASE), jnp.where(place == 1, 1.0, 0.0)).astype(jnp.bfloat16)
    target_copy.wait()
    index_copy.wait()
    for copy in copies:
        copy.wait()
    for k in range(users):
        items[k * stride:k * stride + rows, :] = lax.dot_general(
            table[k * stride + rows:(k + 1) * stride, :rows], units, TN, preferred_element_type=jnp.float32
        )

    def advance(step, _):
        for r in range(peers):
            bases = [index[r * blocks + step, k] for k in range(picks)]
            narrow = block_of(narrows[r], step)
            candidates = gather_slabs(table, bases, per_piece, stride, slab)
            ids = gather_slabs(items, bases, per_piece, stride, slab)
            score = lax.dot_general(candidates, narrow, NT, preferred_element_type=jnp.float32)
            masked = jnp.where(ids == labels[pl.ds(r * blocks + step, 1), :], -1e30, score)
            scores[step, r] = masked
            peak = jnp.max(masked, axis=0, keepdims=True)
            total = jnp.sum(jnp.exp(masked - peak), axis=0, keepdims=True)
            if r == 0:
                positive = lane_row(narrow.astype(jnp.float32) * block_of(target, step).astype(jnp.float32))
                stats[pl.ds(kept + step, 1), :] = positive
                higher = jnp.maximum(peak, positive)
                total = total * jnp.exp(peak - higher) + jnp.exp(positive - higher)
                peak = higher
            stats[pl.ds(r * blocks + step, 1), :] = peak
            stats[pl.ds((peers + r) * blocks + step, 1), :] = total
        return 0

    lax.fori_loop(0, blocks, advance, 0, unroll=2)


def tree_sum(terms):
    while len(terms) > 1:
        terms = [terms[k] + terms[k + 1] for k in range(0, len(terms), 2)]
    return terms[0]


def grad_kernel(dims, index, *refs):
    peers, blocks, picks, users, per_piece, slab, factor = dims
    scores, weights, table = refs[:3]
    stats = refs[3:3 + peers]
    outs = refs[3 + peers:]
    near, far, pos_grad, word = outs[:4]
    hiddens, (peaks, ratios) = outs[4:3 + peers], outs[3 + peers:]
    kept = 2 * peers * blocks
    stride = per_piece * slab + HEAD

    terms = []
    for r in range(peers):
        tops = [stats[q][pl.ds((q ^ r) * blocks, blocks), :] for q in range(peers)]
        sums = [stats[q][pl.ds((peers + (q ^ r)) * blocks, blocks), :] for q in range(peers)]
        peak = functools.reduce(jnp.maximum, tops)
        total = tree_sum([s * jnp.exp(t - peak) for t, s in zip(tops, sums)])
        weight = weights[r * blocks:(r + 1) * blocks, :]
        peaks[r * blocks:(r + 1) * blocks, :] = peak
        ratios[r * blocks:(r + 1) * blocks, :] = weight * factor / total
        positive = stats[r][pl.ds(kept, blocks), :]
        terms.append(weight * (peak + jnp.log(total) - positive))
        if r == 0:
            pos_grad[...] = weight * factor * (jnp.exp(positive - peak) / total - 1.0)
    word[:4, :] = jnp.broadcast_to(jnp.sum(tree_sum(terms), keepdims=True) * factor, (4, word.shape[1]))
    top = jnp.maximum(stats[0][pl.ds(kept + blocks, 4), :], 1e-30)
    word[4:, :] = top

    def advance(step, _):
        span = pl.ds(pl.multiple_of(step * PB, PB), PB)
        for r in range(peers):
            peak = peaks[pl.ds(r * blocks + step, 1), :]
            ratio = ratios[pl.ds(r * blocks + step, 1), :]
            grad = (jnp.exp(scores[step, r] - peak) * ratio).astype(jnp.bfloat16)
            if r == 0:
                near[step] = grad
            else:
                far[step, r - 1] = grad
                bases = [index[r * blocks + step, k] for k in range(picks)]
                candidates = gather_slabs(table, bases, per_piece, stride, slab)
                hiddens[r - 1][span, :] = lax.dot_general(grad, candidates, TN, preferred_element_type=jnp.float32)
        return 0

    lax.fori_loop(0, blocks, advance, 0, unroll=2)


def table_kernel(dims, index, *refs):
    peers, blocks, picks, users, per_piece, slab = dims
    near, far = refs[:2]
    narrows = refs[2:2 + peers]
    partial = refs[2 + peers]
    partial[...] = jnp.zeros_like(partial)

    def advance(step, _):
        for r in range(peers):
            grad = near[step] if r == 0 else far[step, r - 1]
            rows = jnp.dot(grad, block_of(narrows[r], step), preferred_element_type=jnp.float32)
            for k in range(picks):
                place = pl.ds(pl.multiple_of(index[r * blocks + step, k] * slab, 16), slab)
                partial[place, :] += rows[k * slab:(k + 1) * slab]
        return 0

    lax.fori_loop(0, blocks, advance, 0, unroll=2)


def hidden_kernel(dims, index, near, table, pos_grad, target, from_core, out):
    peers, blocks, picks, users, per_piece, slab = dims
    stride = per_piece * slab + HEAD

    def advance(step, _):
        span = pl.ds(pl.multiple_of(step * PB, PB), PB)
        candidates = gather_slabs(table, [index[step, k] for k in range(picks)], per_piece, stride, slab)
        result = lax.dot_general(near[step], candidates, TN, preferred_element_type=jnp.float32)
        row = jnp.broadcast_to(pos_grad[pl.ds(step, 1), :], (PB, PB)).T
        wide = block_of(target, step).astype(jnp.float32)
        for k in range(0, wide.shape[1], PB):
            out[span, k:k + PB] = result[:, k:k + PB] + row * wide[:, k:k + PB] + from_core[span, k:k + PB]
        return 0

    lax.fori_loop(0, blocks, advance, 0, unroll=2)


def order_kernel(dims, rank, *refs):
    peers, blocks, picks, users, per_piece, slab = dims
    quarters, out, sems = refs[:peers], refs[peers], refs[peers + 1]
    copies = []
    for q, quarter in enumerate(quarters):
        for k in range(per_piece):
            place = pl.multiple_of(k * NB + (rank[0] ^ q) * slab, slab)
            copies.append(pltpu.make_async_copy(
                quarter.at[pl.ds(k * slab, slab)], out.at[pl.ds(place, slab)], sems.at[q * per_piece + k]
            ))
    for copy in copies:
        copy.start()
    for copy in copies:
        copy.wait()


def per_device(hidden, target, pool_table, pool_items, labels, chosen, offsets):
    users, peers = lax.axis_size("users"), lax.axis_size("seq")
    user, peer = lax.axis_index("users"), lax.axis_index("seq")
    length, features = hidden.shape[1], hidden.shape[2]
    blocks, picks = length // PB, chosen.shape[2]
    per_piece = pool_table.shape[0] // NB
    slab = NB // peers
    rows = per_piece * slab
    stride = rows + HEAD
    wide = picks * slab
    factor = 1.0 / (users * (offsets.shape[1] - 1))
    f32, bf16 = jnp.float32, jnp.bfloat16

    def halves(whole_numbers):
        numbers = whole_numbers.reshape(-1)
        numbers = jnp.pad(numbers, (0, -numbers.shape[0] % features)).reshape(-1, features)
        return [(numbers // ID_BASE).astype(bf16), (numbers % ID_BASE).astype(bf16)]

    own_rows = lax.dynamic_slice_in_dim(pool_table.reshape(per_piece, NB, features), peer * slab, slab, axis=1)
    own_ids = lax.dynamic_slice_in_dim(pool_items.reshape(per_piece, NB), peer * slab, slab, axis=1)
    spare = jnp.zeros((HEAD - 2, features), bf16)
    piece = jnp.concatenate([own_rows.reshape(rows, features)] + halves(own_ids) + [spare])

    in_vmem, in_smem = pl.BlockSpec(memory_space=pltpu.VMEM), pl.BlockSpec(memory_space=pltpu.SMEM)
    in_hbm = pl.BlockSpec(memory_space=pltpu.HBM)
    params = pltpu.CompilerParams(vmem_limit_bytes=VMEM)
    _, first_lot, note_rows = note_places(length, features, blocks)
    packed = pl.pallas_call(
        pack_kernel,
        in_specs=[in_hbm] * 3,
        out_specs=in_vmem,
        out_shape=jax.ShapeDtypeStruct((length + note_rows, features), bf16),
        scratch_shapes=[
            pltpu.VMEM(labels.shape, jnp.int32),
            pltpu.VMEM(chosen.shape[1:], jnp.int32),
            pltpu.VMEM((length, features), f32),
            pltpu.VMEM((blocks, features), f32),
            pltpu.SemaphoreType.DMA((4,)),
            pltpu.SemaphoreType.DMA((2,)),
        ],
        compiler_params=params, name="states",
    )(*[pltpu.with_memory_space_constraint(x, pltpu.HBM) for x in (labels, chosen[0], hidden[0])])

    pieces = {0: piece, 1: swap(piece, "users", 1)}
    states = {0: packed}
    for q in range(2, peers, 2):
        states[q] = swap(packed, "seq", q)
    pairs = users // 2
    if pairs == 4:
        pieces[4], pieces[2] = swap(piece, "users", 4), swap(piece, "users", 2)
        pieces = lax.optimization_barrier(pieces)
        pieces[6], pieces[5] = swap(pieces[4], "users", 2), swap(pieces[4], "users", 1)
        pieces = lax.optimization_barrier(pieces)
        own, came = lax.optimization_barrier((packed, pieces[6]))
        pieces[7], pieces[3] = swap(pieces[6], "users", 1), swap(pieces[1], "users", 2)
    else:
        for q in range(2, users, 2):
            pieces[q] = swap(piece, "users", q)
            pieces[q + 1] = swap(pieces[q], "users", 1)
        own = packed
    states[1] = swap(own, "seq", 1)
    for q in range(2, peers, 2):
        states[q + 1] = swap(states[q], "seq", 1)
    narrows = [states[q] for q in range(peers)]
    pieces = [pieces[q] for q in range(users)]

    owners = peer ^ jnp.arange(peers, dtype=jnp.int32)
    positions = owners[:, None] * length + jnp.arange(length, dtype=jnp.int32)[None, :]
    weights = history_weights(offsets[0], positions).reshape(peers * blocks, PB)
    weights, narrows = lax.optimization_barrier((weights, narrows))

    dims = (peers, blocks, picks, users, per_piece, slab)
    half = features // 2
    stat_rows = (2 * peers + 1) * blocks + 8
    cost = pl.CostEstimate(flops=1 << 20, bytes_accessed=1 << 20, transcendentals=0)

    def call(kernel, name, outs, scratch, rows_of, *operands, unplaced=0):
        placed = len(operands) - unplaced
        return pl.pallas_call(
            kernel,
            in_specs=[in_smem] + [in_vmem] * placed + [in_hbm] * unplaced,
            out_specs=[in_smem if dtype == jnp.int32 else in_vmem for _, dtype in outs],
            out_shape=[jax.ShapeDtypeStruct(shape, dtype) for shape, dtype in outs],
            scratch_shapes=scratch,
            compiler_params=params, cost_estimate=cost, name=name,
        )(rows_of, *operands[:placed], *[pltpu.with_memory_space_constraint(x, pltpu.HBM) for x in operands[placed:]])

    scores, stats, table, index = call(
        functools.partial(score_kernel, dims), "scores",
        [
            ((blocks, peers, wide, PB), f32), ((stat_rows, PB), f32), ((users * stride, features), bf16),
            ((peers * blocks, PB), jnp.int32),
        ],
        [
            pltpu.VMEM((users * stride, PB), f32),
            pltpu.VMEM((length, features), bf16),
            pltpu.VMEM((peers * blocks, PB), f32),
            pltpu.VMEM((peers * blocks, PB), jnp.int32),
            pltpu.SemaphoreType.DMA((users,)),
            pltpu.SemaphoreType.DMA,
            pltpu.SemaphoreType.DMA,
        ],
        user.reshape(1), *narrows, target[0], *pieces, unplaced=1 + users,
    )
    all_stats = [stats] + [swap(stats, "seq", q) for q in range(1, peers)]

    state_out = ((length, features), f32)
    near, far, pos_grad, word, *hiddens = call(
        functools.partial(grad_kernel, dims + (factor,)), "grads",
        [
            ((blocks, wide, PB), bf16),
            ((blocks, peers - 1, wide, PB), bf16),
            ((blocks, PB), f32),
            ((8, PB), f32),
        ] + [state_out] * (peers - 1),
        [pltpu.VMEM((peers * blocks, PB), f32)] * 2,
        index, scores, weights, table, *all_stats,
    )

    def meet(ours, theirs):
        row = lax.broadcasted_iota(jnp.int32, ours.shape, 0)
        return jnp.where(row < 4, ours + theirs, jnp.maximum(ours, theirs))

    from_core = [swap(hiddens[q], "seq", 1) for q in range(2, peers, 2)]
    partner_word = swap(word, "users", 1)
    (partial,) = call(
        functools.partial(table_kernel, dims), "table_grads", [((users * rows, features), f32)], [],
        index, near, far, *narrows,
    )
    partial, from_core, partner_word = lax.optimization_barrier((partial, from_core, partner_word))

    hidden_scale = 16384.0 / factor

    parts = partial.reshape(users, rows, features)
    halved = [slice(0, half), slice(half, features)]

    def coded(sums, bound):
        return (sums * (16384.0 / bound)).astype(jnp.float16)

    def added(sums, *arrived):
        for part, bound in arrived:
            sums = sums + part.astype(f32) * (bound / 16384.0)
        return sums

    def bound_of(word):
        row = jnp.maximum(word[4:5], 1e-30)
        return jnp.concatenate([row] * (features // PB), axis=1)

    def coded_hiddens(lanes):
        return [
            ((hiddens[2 * k + 1][:, lanes] + part[:, lanes]) * hidden_scale).astype(jnp.float16)
            for k, part in enumerate(from_core)
        ]

    def with_far(coded):
        return [swap(part, "seq", 2 * k + 2) for k, part in enumerate(coded)]

    word = meet(word, partner_word)
    if pairs == 4:
        pair_bound = bound_of(word)
        sent, hidden_coded = lax.optimization_barrier(
            ([coded(parts[7], pair_bound), coded(parts[3], pair_bound)], coded_hiddens(halved[0]))
        )
        from_pair, from_line = swap(sent[0], "users", 1), swap(sent[1], "users", 2)
        hidden_arrived = [with_far(hidden_coded)]
        line_word = swap(word, "users", 2)
        own_core = swap(hiddens[0], "seq", 1)
        from_pair, from_line, line_word = lax.optimization_barrier((from_pair, from_line, line_word))
        line_bound, word = bound_of(line_word), meet(word, line_word)
        four_bound = bound_of(word)
        pair_sum = added(parts[1], (from_line, line_bound))
        sent = [coded(added(parts[6], (from_pair, pair_bound)), four_bound), coded(parts[5], four_bound)]

        from_line, from_pair = swap(sent[0], "users", 2), swap(sent[1], "users", 1)
        far_word = swap(word, "users", 4)
        from_pair, from_line, far_word, hidden_arrived, own_core, hidden_coded, near = lax.optimization_barrier(
            (from_pair, from_line, far_word, hidden_arrived, own_core, coded_hiddens(halved[1]), near)
        )
        word = meet(word, far_word)
        top = bound_of(word)
        far_sum = added(parts[4], (from_line, four_bound), (from_pair, four_bound))
        sent = [coded(far_sum, top), coded(parts[2], top), coded(pair_sum, top)]

        arrived = [swap(sent[0], "users", 4), swap(sent[1], "users", 2), swap(sent[2], "users", 1)]
        hidden_arrived.append(with_far(hidden_coded))
        (own_hidden,) = call(
            functools.partial(hidden_kernel, dims), "own_hidden_grads", [state_out], [],
            index, near, table, pos_grad, target[0], own_core,
        )
        arrived, own_hidden, hidden_arrived = lax.optimization_barrier((arrived, own_hidden, hidden_arrived))
        owned = added(parts[0], *[(part, top) for part in arrived])
    else:
        mask = 2
        while mask < users:
            word = meet(word, swap(word, "users", mask))
            mask *= 2
        top = bound_of(word)
        owned = parts[0]
        for q in range(0, users, 2):
            sums = added(parts[q], (swap(coded(parts[q + 1], top), "users", 1), top))
            owned = sums if q == 0 else added(owned, (swap(coded(sums, top), "users", q), top))
        hidden_arrived = [with_far(coded_hiddens(lanes)) for lanes in halved]
        own_core = swap(hiddens[0], "seq", 1)
        (own_hidden,) = call(
            functools.partial(hidden_kernel, dims), "own_hidden_grads", [state_out], [],
            index, near, table, pos_grad, target[0], own_core,
        )

    grad_hidden = own_hidden
    for k in range(peers // 2 - 1):
        part = jnp.concatenate([lanes[k] for lanes in hidden_arrived], axis=1)
        grad_hidden = grad_hidden + part.astype(f32) * (1.0 / hidden_scale)
    quarters = {0: owned, 1: swap(owned, "seq", 1)}
    for q in range(2, peers, 2):
        quarters[q] = swap(coded(owned, top), "seq", q)
    quarters, grad_hidden = lax.optimization_barrier((quarters, grad_hidden))
    for q in range(2, peers, 2):
        far = quarters[q]
        quarters[q], quarters[q + 1] = added(0.0, (far, top)), added(0.0, (swap(far, "seq", 1), top))
    grad_table = pl.pallas_call(
        functools.partial(order_kernel, dims),
        in_specs=[in_smem] + [in_vmem] * peers,
        out_specs=in_hbm,
        out_shape=jax.ShapeDtypeStruct(pool_table.shape, f32),
        scratch_shapes=[pltpu.SemaphoreType.DMA((peers * per_piece,))],
        compiler_params=params, name="ordered_table_grads",
    )(peer.reshape(1), *[quarters[q] for q in range(peers)])
    return word[0, 0], grad_hidden[None], grad_table


def solution(mesh):
    return jax.shard_map(
        per_device,
        mesh=mesh,
        in_specs=(
            P("users", "seq", None),
            P("users", "seq", None),
            P("users", None),
            P("users"),
            P("users", "seq"),
            P("users", "seq", None),
            P("users", None),
        ),
        out_specs=(P(), P("users", "seq", None), P("users", None)),
        check_vma=False,
    )
```

```python
import functools
import jax
import jax.numpy as jnp
from jax import lax
from jax.experimental import pallas as pl
from jax.experimental.pallas import tpu as pltpu
from jax.sharding import PartitionSpec as P

NB = 256
PB = 128
HEAD = 16
ID_BASE = 128
VMEM = 8 * 1024 * 1024
NT = (((1,), (1,)), ((), ()))
TN = (((0,), (0,)), ((), ()))


def swap(array, axis, mask):
    count = lax.axis_size(axis)
    return lax.ppermute(array, axis, [(i, i ^ mask) for i in range(count)])


def history_weights(bounds, positions):
    starts = bounds[:-1]
    finish = bounds[1:]
    lengths = (finish - starts).astype(jnp.float32)
    inside = (positions[..., None] >= starts) & (positions[..., None] < finish)
    return jnp.sum(jnp.where(inside, 1.0 / lengths, 0.0), axis=-1)


def note_places(length, features, blocks):
    lines = length // features
    return lines, 2 * lines, -(-(2 * lines + blocks + 1) // HEAD) * HEAD


def is_late(users, slot):
    return (slot & 3) == 3 if users == 8 else slot < 0


def place_of(users, slot):
    return jnp.where(is_late(users, slot), 6 + (slot >> 2), slot - (slot >> 2)) if users == 8 else slot


def gather_slabs(table, bases, per_piece, stride, slab):
    rows = []
    for base in bases:
        row = (base // per_piece) * stride + (base % per_piece) * slab
        rows.append(table[pl.ds(pl.multiple_of(row, 16), slab), :])
    return jnp.concatenate(rows, axis=0)


def block_of(ref, step):
    return ref[pl.ds(pl.multiple_of(step * PB, PB), PB), :]


def lane_row(columns):
    folded = columns[:, :PB]
    for k in range(1, columns.shape[1] // PB):
        folded = folded + columns[:, k * PB:(k + 1) * PB]
    return jnp.sum(folded.T, axis=0, keepdims=True)


def pack_kernel(users, per_piece, user, labels_from, chosen_from, hidden_from, packed, labels, chosen, hidden, lots, sems, note_sems):
    note_copies = [
        pltpu.make_async_copy(labels_from, labels, note_sems.at[0]),
        pltpu.make_async_copy(chosen_from, chosen, note_sems.at[1]),
    ]
    for copy in note_copies:
        copy.start()
    length, features = hidden.shape
    blocks, picks = chosen.shape
    lines, first, count = note_places(length, features, blocks)
    part = length // sems.shape[0]
    copies = [
        pltpu.make_async_copy(hidden_from.at[pl.ds(k * part, part)], hidden.at[pl.ds(k * part, part)], sems.at[k])
        for k in range(sems.shape[0])
    ]
    for copy in copies:
        copy.start()
    lots[...] = jnp.zeros_like(lots)
    for copy in note_copies:
        copy.wait()
    columns = [chosen[:, k:k + 1] for k in range(picks)]
    late = [is_late(users, (column // per_piece) ^ user[0]).astype(jnp.int32) for column in columns]
    ranks = [
        sum(((late[j] < late[k]) | ((late[j] == late[k]) & (j < k))).astype(jnp.int32) for j in range(picks))
        for k in range(picks)
    ]
    for place in range(picks):
        column = sum(jnp.where(rank == place, column, 0) for rank, column in zip(ranks, columns))
        lots[:, place:place + 1] = column.astype(jnp.float32)
    row = lax.broadcasted_iota(jnp.int32, (count, features), 0)
    notes = jnp.zeros((count, features), jnp.float32)
    for k in range(lines):
        line = labels[:, k * features:(k + 1) * features]
        notes = jnp.where(row == k, (line // ID_BASE).astype(jnp.float32), notes)
        notes = jnp.where(row == lines + k, (line % ID_BASE).astype(jnp.float32), notes)
    for k in range(blocks):
        notes = jnp.where(row == first + k, lots[k:k + 1, :], notes)
    top = jnp.zeros((8, features), jnp.float32)
    for k, copy in enumerate(copies):
        copy.wait()
        narrow = hidden[k * part:(k + 1) * part, :].astype(jnp.bfloat16)
        packed[k * part:(k + 1) * part, :] = narrow
        sizes = jnp.abs(narrow.astype(jnp.float32))
        top = jnp.maximum(top, jnp.max(sizes.reshape(part // 8, 8, features), axis=0))
    notes = jnp.where(row == count - 1, jnp.max(top, keepdims=True), notes)
    packed[length:, :] = notes.astype(jnp.bfloat16)


def load_items(items, table, first, count, rows, stride):
    place = lax.broadcasted_iota(jnp.int32, (HEAD, PB), 0)
    units = jnp.where(place == 0, float(ID_BASE), jnp.where(place == 1, 1.0, 0.0)).astype(jnp.bfloat16)
    for k in range(first, first + count):
        items[k * stride:k * stride + rows, :] = lax.dot_general(
            table[k * stride + rows:(k + 1) * stride, :rows], units, TN, preferred_element_type=jnp.float32
        )


def masked_scores(table, items, bases, narrow, label, per_piece, stride, slab):
    candidates = gather_slabs(table, bases, per_piece, stride, slab)
    ids = gather_slabs(items, bases, per_piece, stride, slab)
    score = lax.dot_general(candidates, narrow, NT, preferred_element_type=jnp.float32)
    return jnp.where(ids == label, -1e30, score)


def early_kernel(dims, user, *refs):
    peers, blocks, picks, users, per_piece, slab = dims
    narrows, target_from, pieces = refs[:peers], refs[peers], refs[1 + peers:-12]
    scores, table, items, index, labels, positives, tops, target, lots, sems, target_sem, index_sem = refs[-12:]
    rows = per_piece * slab
    stride = rows + HEAD
    length, features = target.shape
    lines, first_lot, _ = note_places(length, features, blocks)

    target_copy = pltpu.make_async_copy(target_from, target, target_sem)
    target_copy.start()
    copies = [
        pltpu.make_async_copy(piece, table.at[pl.ds(k * stride, stride)], sems.at[k])
        for k, piece in enumerate(pieces)
    ]
    for copy in copies:
        copy.start()
    largest = []
    for r in range(peers):
        notes = narrows[r][length:, :].astype(jnp.float32)
        lot = notes[first_lot:first_lot + blocks, :PB].astype(jnp.int32)
        slot = place_of(users, (lot // per_piece) ^ user[0])
        lots[r * blocks:(r + 1) * blocks, :] = slot * per_piece + lot % per_piece
        for k in range(blocks):
            line, lane = divmod(k * PB, features)
            high, low = notes[line:line + 1, lane:lane + PB], notes[lines + line:lines + line + 1, lane:lane + PB]
            labels[r * blocks + k:r * blocks + k + 1, :] = high * ID_BASE + low
        largest.append(notes[-1:, :PB])
    index_copy = pltpu.make_async_copy(lots, index, index_sem)
    index_copy.start()
    tops[...] = jnp.broadcast_to(functools.reduce(jnp.maximum, largest), (8, PB))
    target_copy.wait()
    index_copy.wait()
    for copy in copies:
        copy.wait()
    load_items(items, table, 0, len(pieces), rows, stride)
    last = len(pieces) * per_piece - 1

    def advance(step, _):
        for r in range(peers):
            row = r * blocks + step
            bases = [jnp.minimum(index[row, k], last) for k in range(picks // 2)]
            narrow = block_of(narrows[r], step)
            label = labels[pl.ds(row, 1), :]
            scores[step, r] = masked_scores(table, items, bases, narrow, label, per_piece, stride, slab)
            if r == 0:
                product = narrow.astype(jnp.float32) * block_of(target, step).astype(jnp.float32)
                positives[pl.ds(step, 1), :] = lane_row(product)
        return 0

    lax.fori_loop(0, blocks, advance, 0, unroll=4)


def late_kernel(dims, index, *refs):
    peers, blocks, picks, users, per_piece, slab = dims
    narrows = refs[:peers]
    first_scores, first_table, first_items, labels, positives = refs[peers:peers + 5]
    pieces = refs[peers + 5:-5]
    scores, stats, table, items, sems = refs[-5:]
    rows = per_piece * slab
    stride = rows + HEAD
    kept = 2 * peers * blocks
    half = picks // 2
    middle = half * slab
    early = first_table.shape[0] // stride

    copies = [
        pltpu.make_async_copy(piece, table.at[pl.ds((early + k) * stride, stride)], sems.at[k])
        for k, piece in enumerate(pieces)
    ]
    for copy in copies:
        copy.start()
    table[:early * stride, :] = first_table[...]
    items[:early * stride, :] = first_items[...]
    stats[pl.ds(kept, blocks), :] = positives[...]

    for copy in copies:
        copy.wait()
    load_items(items, table, early, len(pieces), rows, stride)

    def summarise(row, first, second, positive):
        peak = jnp.maximum(jnp.max(first, axis=0, keepdims=True), jnp.max(second, axis=0, keepdims=True))
        total = jnp.sum(jnp.exp(first - peak) + jnp.exp(second - peak), axis=0, keepdims=True)
        if positive is not None:
            higher = jnp.maximum(peak, positive)
            total = total * jnp.exp(peak - higher) + jnp.exp(positive - higher)
            peak = higher
        stats[pl.ds(row, 1), :] = peak
        stats[pl.ds(peers * blocks + row, 1), :] = total

    def advance(step, _):
        for r in range(peers):
            row = r * blocks + step
            bases = [index[row, k] for k in range(half, picks)]
            label = labels[pl.ds(row, 1), :]
            second = masked_scores(
                table, items, bases, block_of(narrows[r], step), label, per_piece, stride, slab
            )
            first = first_scores[step, r]
            scores[step, r, :middle, :] = first
            scores[step, r, middle:, :] = second
            summarise(row, first, second, positives[pl.ds(step, 1), :] if r == 0 else None)
        return 0

    lax.fori_loop(0, blocks, advance, 0, unroll=4)

    if pieces:
        def repair(row, _):
            @pl.when(index[row, half - 1] >= early * per_piece)
            def _():
                step = row % blocks
                bases = [index[row, k] for k in range(half)]
                label = labels[pl.ds(row, 1), :]
                for r in range(peers):
                    @pl.when(row // blocks == r)
                    def _(r=r):
                        first = masked_scores(
                            table, items, bases, block_of(narrows[r], step), label, per_piece, stride, slab
                        )
                        scores[step, r, :middle, :] = first
                        second = scores[step, r, middle:, :]
                        summarise(row, first, second, positives[pl.ds(step, 1), :] if r == 0 else None)
            return 0

        lax.fori_loop(0, peers * blocks, repair, 0)


def tree_sum(terms):
    while len(terms) > 1:
        terms = [terms[k] + terms[k + 1] for k in range(0, len(terms), 2)]
    return terms[0]


def grad_kernel(dims, index, *refs):
    peers, blocks, picks, users, per_piece, slab, factor = dims
    scores, weights, table = refs[:3]
    stats = refs[3:3 + peers]
    largest, partner_largest = refs[3 + peers:5 + peers]
    outs = refs[5 + peers:]
    near, far, pos_grad, word = outs[:4]
    hiddens, (peaks, ratios) = outs[4:3 + peers], outs[3 + peers:]
    kept = 2 * peers * blocks
    stride = per_piece * slab + HEAD

    terms = []
    for r in range(peers):
        tops = [stats[q][pl.ds((q ^ r) * blocks, blocks), :] for q in range(peers)]
        sums = [stats[q][pl.ds((peers + (q ^ r)) * blocks, blocks), :] for q in range(peers)]
        peak = functools.reduce(jnp.maximum, tops)
        total = tree_sum([s * jnp.exp(t - peak) for t, s in zip(tops, sums)])
        weight = weights[r * blocks:(r + 1) * blocks, :]
        peaks[r * blocks:(r + 1) * blocks, :] = peak
        ratios[r * blocks:(r + 1) * blocks, :] = weight * factor / total
        positive = stats[r][pl.ds(kept, blocks), :]
        terms.append(weight * (peak + jnp.log(total) - positive))
        if r == 0:
            pos_grad[...] = weight * factor * (jnp.exp(positive - peak) / total - 1.0)
    word[:4, :] = jnp.broadcast_to(jnp.sum(tree_sum(terms), keepdims=True) * factor, (4, word.shape[1]))
    word[4:, :] = jnp.maximum(jnp.maximum(largest[4:, :], partner_largest[4:, :]), 1e-30)

    def advance(step, _):
        span = pl.ds(pl.multiple_of(step * PB, PB), PB)
        for r in range(peers):
            peak = peaks[pl.ds(r * blocks + step, 1), :]
            ratio = ratios[pl.ds(r * blocks + step, 1), :]
            grad = (jnp.exp(scores[step, r] - peak) * ratio).astype(jnp.bfloat16)
            if r == 0:
                near[step] = grad
            else:
                far[step, r - 1] = grad
                bases = [index[r * blocks + step, k] for k in range(picks)]
                candidates = gather_slabs(table, bases, per_piece, stride, slab)
                hiddens[r - 1][span, :] = lax.dot_general(grad, candidates, TN, preferred_element_type=jnp.float32)
        return 0

    lax.fori_loop(0, blocks, advance, 0, unroll=8)


def table_kernel(dims, index, *refs):
    peers, blocks, picks, users, per_piece, slab = dims
    near, far = refs[:2]
    narrows = refs[2:2 + peers]
    partial = refs[2 + peers]
    partial[...] = jnp.zeros_like(partial)

    def advance(step, _):
        for r in range(peers):
            grad = near[step] if r == 0 else far[step, r - 1]
            rows = jnp.dot(grad, block_of(narrows[r], step), preferred_element_type=jnp.float32)
            for k in range(picks):
                place = pl.ds(pl.multiple_of(index[r * blocks + step, k] * slab, 16), slab)
                partial[place, :] += rows[k * slab:(k + 1) * slab]
        return 0

    lax.fori_loop(0, blocks, advance, 0, unroll=4)


def hidden_kernel(dims, index, near, table, pos_grad, target, from_core, out):
    peers, blocks, picks, users, per_piece, slab = dims
    stride = per_piece * slab + HEAD

    def advance(step, _):
        span = pl.ds(pl.multiple_of(step * PB, PB), PB)
        candidates = gather_slabs(table, [index[step, k] for k in range(picks)], per_piece, stride, slab)
        result = lax.dot_general(near[step], candidates, TN, preferred_element_type=jnp.float32)
        row = jnp.broadcast_to(pos_grad[pl.ds(step, 1), :], (PB, PB)).T
        wide = block_of(target, step).astype(jnp.float32)
        for k in range(0, wide.shape[1], PB):
            out[span, k:k + PB] = result[:, k:k + PB] + row * wide[:, k:k + PB] + from_core[span, k:k + PB]
        return 0

    lax.fori_loop(0, blocks, advance, 0, unroll=8)


def order_kernel(dims, rank, *refs):
    peers, blocks, picks, users, per_piece, slab = dims
    quarters, out, sems = refs[:peers], refs[peers], refs[peers + 1]
    copies = []
    for q, quarter in enumerate(quarters):
        for k in range(per_piece):
            place = pl.multiple_of(k * NB + (rank[0] ^ q) * slab, slab)
            copies.append(pltpu.make_async_copy(
                quarter.at[pl.ds(k * slab, slab)], out.at[pl.ds(place, slab)], sems.at[q * per_piece + k]
            ))
    for copy in copies:
        copy.start()
    for copy in copies:
        copy.wait()


def per_device(hidden, target, pool_table, pool_items, labels, chosen, offsets):
    users, peers = lax.axis_size("users"), lax.axis_size("seq")
    user, peer = lax.axis_index("users"), lax.axis_index("seq")
    length, features = hidden.shape[1], hidden.shape[2]
    blocks, picks = length // PB, chosen.shape[2]
    per_piece = pool_table.shape[0] // NB
    slab = NB // peers
    rows = per_piece * slab
    stride = rows + HEAD
    wide = picks * slab
    factor = 1.0 / (users * (offsets.shape[1] - 1))
    f32, bf16 = jnp.float32, jnp.bfloat16

    def halves(whole_numbers):
        numbers = whole_numbers.reshape(-1)
        numbers = jnp.pad(numbers, (0, -numbers.shape[0] % features)).reshape(-1, features)
        return [(numbers // ID_BASE).astype(bf16), (numbers % ID_BASE).astype(bf16)]

    own_rows = lax.dynamic_slice_in_dim(pool_table.reshape(per_piece, NB, features), peer * slab, slab, axis=1)
    own_ids = lax.dynamic_slice_in_dim(pool_items.reshape(per_piece, NB), peer * slab, slab, axis=1)
    spare = jnp.zeros((HEAD - 2, features), bf16)
    piece = jnp.concatenate([own_rows.reshape(rows, features)] + halves(own_ids) + [spare])

    in_vmem, in_smem = pl.BlockSpec(memory_space=pltpu.VMEM), pl.BlockSpec(memory_space=pltpu.SMEM)
    in_hbm = pl.BlockSpec(memory_space=pltpu.HBM)
    params = pltpu.CompilerParams(vmem_limit_bytes=VMEM)
    _, first_lot, note_rows = note_places(length, features, blocks)
    packed = pl.pallas_call(
        functools.partial(pack_kernel, users, per_piece),
        in_specs=[in_smem] + [in_hbm] * 3,
        out_specs=in_vmem,
        out_shape=jax.ShapeDtypeStruct((length + note_rows, features), bf16),
        scratch_shapes=[
            pltpu.VMEM(labels.shape, jnp.int32),
            pltpu.VMEM(chosen.shape[1:], jnp.int32),
            pltpu.VMEM((length, features), f32),
            pltpu.VMEM((blocks, features), f32),
            pltpu.SemaphoreType.DMA((4,)),
            pltpu.SemaphoreType.DMA((2,)),
        ],
        compiler_params=params, name="states",
    )(user.reshape(1), *[pltpu.with_memory_space_constraint(x, pltpu.HBM) for x in (labels, chosen[0], hidden[0])])

    pairs = users // 2
    pieces, states = {0: piece}, {0: packed}
    for q in (4, 2, 1) if pairs == 4 else (1,):
        pieces[q] = swap(piece, "users", q)
    for q in range(2, peers, 2):
        states[q] = swap(packed, "seq", q)
    if pairs == 4:
        pieces[4], pieces[2], pieces[1] = lax.optimization_barrier((pieces[4], pieces[2], pieces[1]))
        pieces[6], pieces[5] = swap(pieces[4], "users", 2), swap(pieces[4], "users", 1)
        pieces[6], pieces[5], pieces[1], own = lax.optimization_barrier((pieces[6], pieces[5], pieces[1], packed))
        pieces[7], pieces[3] = swap(pieces[6], "users", 1), swap(pieces[1], "users", 2)
    else:
        for q in range(2, users, 2):
            pieces[q] = swap(piece, "users", q)
            pieces[q + 1] = swap(pieces[q], "users", 1)
        own = packed
    states[1] = swap(own, "seq", 1)
    for q in range(2, peers, 2):
        states[q + 1] = swap(states[q], "seq", 1)
    narrows = [states[q] for q in range(peers)]
    pieces = [pieces[q] for q in range(users)]

    owners = peer ^ jnp.arange(peers, dtype=jnp.int32)
    positions = owners[:, None] * length + jnp.arange(length, dtype=jnp.int32)[None, :]
    weights = history_weights(offsets[0], positions).reshape(peers * blocks, PB)
    weights, narrows = lax.optimization_barrier((weights, narrows))

    dims = (peers, blocks, picks, users, per_piece, slab)
    half = features // 2
    stat_rows = (2 * peers + 1) * blocks
    cost = pl.CostEstimate(flops=1 << 20, bytes_accessed=1 << 20, transcendentals=0)

    def call(kernel, name, outs, scratch, rows_of, *operands, unplaced=0):
        placed = len(operands) - unplaced
        return pl.pallas_call(
            kernel,
            in_specs=[in_smem] + [in_vmem] * placed + [in_hbm] * unplaced,
            out_specs=[in_smem if dtype == jnp.int32 else in_vmem for _, dtype in outs],
            out_shape=[jax.ShapeDtypeStruct(shape, dtype) for shape, dtype in outs],
            scratch_shapes=scratch,
            compiler_params=params, cost_estimate=cost, name=name,
        )(rows_of, *operands[:placed], *[pltpu.with_memory_space_constraint(x, pltpu.HBM) for x in operands[placed:]])

    early = [q for q in range(users) if not is_late(users, q)]
    late = [q for q in range(users) if is_late(users, q)]
    first_scores, first_table, first_items, index, label_rows, positives, tops = call(
        functools.partial(early_kernel, dims), "early_scores",
        [
            ((blocks, peers, wide // 2, PB), f32),
            ((len(early) * stride, features), bf16),
            ((len(early) * stride, PB), f32),
            ((peers * blocks, PB), jnp.int32),
            ((peers * blocks, PB), f32),
            ((blocks, PB), f32),
            ((8, PB), f32),
        ],
        [
            pltpu.VMEM((length, features), bf16),
            pltpu.VMEM((peers * blocks, PB), jnp.int32),
            pltpu.SemaphoreType.DMA((len(early),)),
            pltpu.SemaphoreType.DMA,
            pltpu.SemaphoreType.DMA,
        ],
        user.reshape(1), *narrows, target[0], *[pieces[q] for q in early], unplaced=1 + len(early),
    )
    scores, stats, table = call(
        functools.partial(late_kernel, dims), "late_scores",
        [
            ((blocks, peers, wide, PB), f32), ((stat_rows, PB), f32), ((users * stride, features), bf16),
        ],
        [pltpu.VMEM((users * stride, PB), f32), pltpu.SemaphoreType.DMA((max(len(late), 1),))],
        index, *narrows, first_scores, first_table, first_items, label_rows, positives,
        *[pieces[q] for q in late], unplaced=len(late),
    )
    partner_tops = swap(tops, "users", 1)
    all_stats = [stats] + [swap(stats, "seq", q) for q in range(1, peers)]

    state_out = ((length, features), f32)
    near, far, pos_grad, word, *hiddens = call(
        functools.partial(grad_kernel, dims + (factor,)), "grads",
        [
            ((blocks, wide, PB), bf16),
            ((blocks, peers - 1, wide, PB), bf16),
            ((blocks, PB), f32),
            ((8, PB), f32),
        ] + [state_out] * (peers - 1),
        [pltpu.VMEM((peers * blocks, PB), f32)] * 2,
        index, scores, weights, table, *all_stats, tops, partner_tops,
    )

    def meet(ours, theirs):
        row = lax.broadcasted_iota(jnp.int32, ours.shape, 0)
        return jnp.where(row < 4, ours + theirs, jnp.maximum(ours, theirs))

    from_core = [swap(hiddens[q], "seq", 1) for q in range(2, peers, 2)]
    (partial,) = call(
        functools.partial(table_kernel, dims), "table_grads", [((users * rows, features), f32)], [],
        index, near, far, *narrows,
    )
    partial, from_core = lax.optimization_barrier((partial, from_core))

    hidden_scale = 16384.0 / factor

    parts = partial.reshape(users, rows, features)
    parts = {q: parts[k] for k, q in enumerate(early + late)}
    halved = [slice(0, half), slice(half, features)]

    def coded(sums, bound):
        return (sums * (16384.0 / bound)).astype(jnp.float16)

    def added(sums, *arrived):
        for part, bound in arrived:
            sums = sums + part.astype(f32) * (bound / 16384.0)
        return sums

    def bound_of(word):
        row = jnp.maximum(word[4:5], 1e-30)
        return jnp.concatenate([row] * (features // PB), axis=1)

    def coded_hiddens(lanes):
        return [
            ((hiddens[2 * k + 1][:, lanes] + part[:, lanes]) * hidden_scale).astype(jnp.float16)
            for k, part in enumerate(from_core)
        ]

    def with_far(coded):
        return [swap(part, "seq", 2 * k + 2) for k, part in enumerate(coded)]

    if pairs == 4:
        pair_bound = bound_of(word)
        sent, hidden_coded = lax.optimization_barrier(
            ([coded(parts[7], pair_bound), coded(parts[3], pair_bound)], coded_hiddens(halved[0]))
        )
        from_pair, from_line = swap(sent[0], "users", 1), swap(sent[1], "users", 2)
        hidden_arrived = [with_far(hidden_coded)]
        line_word = swap(word, "users", 2)
        own_core = swap(hiddens[0], "seq", 1)
        from_pair, from_line, line_word = lax.optimization_barrier((from_pair, from_line, line_word))
        line_bound, word = bound_of(line_word), meet(word, line_word)
        four_bound = bound_of(word)
        pair_sum = added(parts[1], (from_line, line_bound))
        sent = [coded(added(parts[6], (from_pair, pair_bound)), four_bound), coded(parts[5], four_bound)]
        sent, word = lax.optimization_barrier((sent, word))

        from_line, from_pair = swap(sent[0], "users", 2), swap(sent[1], "users", 1)
        far_word = swap(word, "users", 4)
        from_pair, from_line, far_word, hidden_arrived, own_core, hidden_coded, near = lax.optimization_barrier(
            (from_pair, from_line, far_word, hidden_arrived, own_core, coded_hiddens(halved[1]), near)
        )
        word = meet(word, far_word)
        top = bound_of(word)
        far_sum = added(parts[4], (from_line, four_bound), (from_pair, four_bound))
        sent = [coded(far_sum, top), coded(parts[2], top), coded(pair_sum, top)]

        arrived = [swap(sent[0], "users", 4), swap(sent[1], "users", 2), swap(sent[2], "users", 1)]
        hidden_arrived.append(with_far(hidden_coded))
        last_word = swap(word, "users", 1)
        (own_hidden,) = call(
            functools.partial(hidden_kernel, dims), "own_hidden_grads", [state_out], [],
            index, near, table, pos_grad, target[0], own_core,
        )
        arrived, own_hidden, hidden_arrived, last_word = lax.optimization_barrier(
            (arrived, own_hidden, hidden_arrived, last_word)
        )
        word = meet(word, last_word)
        owned = added(parts[0], *[(part, top) for part in arrived])
    else:
        mask = 1
        while mask < users:
            word = meet(word, swap(word, "users", mask))
            mask *= 2
        top = bound_of(word)
        owned = parts[0]
        for q in range(0, users, 2):
            sums = added(parts[q], (swap(coded(parts[q + 1], top), "users", 1), top))
            owned = sums if q == 0 else added(owned, (swap(coded(sums, top), "users", q), top))
        hidden_arrived = [with_far(coded_hiddens(lanes)) for lanes in halved]
        own_core = swap(hiddens[0], "seq", 1)
        (own_hidden,) = call(
            functools.partial(hidden_kernel, dims), "own_hidden_grads", [state_out], [],
            index, near, table, pos_grad, target[0], own_core,
        )

    grad_hidden = own_hidden
    for k in range(peers // 2 - 1):
        part = jnp.concatenate([lanes[k] for lanes in hidden_arrived], axis=1)
        grad_hidden = grad_hidden + part.astype(f32) * (1.0 / hidden_scale)
    quarters = {0: owned, 1: swap(owned, "seq", 1)}
    for q in range(2, peers, 2):
        quarters[q] = swap(coded(owned, top), "seq", q)
    quarters, grad_hidden = lax.optimization_barrier((quarters, grad_hidden))
    for q in range(2, peers, 2):
        far = quarters[q]
        quarters[q], quarters[q + 1] = added(0.0, (far, top)), added(0.0, (swap(far, "seq", 1), top))
    grad_table = pl.pallas_call(
        functools.partial(order_kernel, dims),
        in_specs=[in_smem] + [in_vmem] * peers,
        out_specs=in_hbm,
        out_shape=jax.ShapeDtypeStruct(pool_table.shape, f32),
        scratch_shapes=[pltpu.SemaphoreType.DMA((peers * per_piece,))],
        compiler_params=params, name="ordered_table_grads",
    )(peer.reshape(1), *[quarters[q] for q in range(peers)])
    return word[0, 0], grad_hidden[None], grad_table


def solution(mesh):
    return jax.shard_map(
        per_device,
        mesh=mesh,
        in_specs=(
            P("users", "seq", None),
            P("users", "seq", None),
            P("users", None),
            P("users"),
            P("users", "seq"),
            P("users", "seq", None),
            P("users", None),
        ),
        out_specs=(P(), P("users", "seq", None), P("users", None)),
        check_vma=False,
    )
```
